256 devices in a mesh: real: 4 (over x), cell: 64 (over y, z, core).
Axes of the slice: x: 4, y: 4, z: 8, core: 2. Of those that a mesh axis runs over, the one named last changes fastest.
Arguments:
- soil_heat_field: float32 [2048, 256, 512], P('cell', None, 'real'), may hold values from -250 to 250, as said below
- seed_subspace: float32 [512, 128], replicated, may hold values from -6 to 6
Outputs:
- core_tensor: float32 [2048, 256, 128], P('cell', None, 'real')
- mode_factor: float32 [512, 128], replicated
- triangle: float32 [512, 512], replicated
The draws below stay inside these ranges and needn't reach their ends.
Inputs may be any that keep to these rules, and one draw needn't show every extreme that they name: `soil_heat_field`: real values.
All inputs are finite; a program needn't handle non-finite values.
Results may differ from the reference program's by a relative error of at most 0.00024.
Values sent between devices are 32-bit elements; how exact they have to be, the bound alone decides.
No kernel may reach another device: no remote copies, remote signals or barrier semaphores. Data moves between devices by JAX's collectives and lax.ppermute only.
A program may use at most 64 MiB of HBM per device.

```python
import math
import jax
import jax.numpy as jnp
from jax import lax

ENSEMBLE_MEMBERS = 512
RANK = 128
SNAPS = 256
ITERS = 3
CELLS = 2048


def draw_soil_heat_field(key, part):
    noise_key = jax.random.fold_in(key, 11)
    scale_key = jax.random.fold_in(key, 23)
    field_key = jax.random.fold_in(key, 37)
    loading_key = jax.random.fold_in(key, 41)
    column_scale = jnp.exp(jax.random.uniform(scale_key, (ENSEMBLE_MEMBERS,), jnp.float32, 0.0, math.log(4.0)))
    position = jnp.arange(CELLS, dtype=jnp.float32) / max(CELLS - 1, 1)
    noise_component = jnp.clip(jax.random.normal(noise_key, (CELLS, SNAPS, ENSEMBLE_MEMBERS), jnp.float32), -4.5, 4.5)
    fields = jnp.clip(jax.random.normal(field_key, (4, CELLS, SNAPS), jnp.float32), -3.0, 3.0)
    loadings = jnp.clip(jax.random.normal(loading_key, (4, ENSEMBLE_MEMBERS), jnp.float32), -3.0, 3.0)
    grid_position_series = 1.0 + 2.0 * position
    blended = noise_component + 0.6 * jnp.roll(noise_component, 1, axis=2)
    for factor_index in range(4):
        blended = blended + 0.15 * fields[factor_index][:, :, None] * loadings[factor_index][None, None, :]
    return blended * grid_position_series[:, None, None] * column_scale[None, None, :]


def normal_values(stream_key, dims, deviation, reach, held_as=jnp.bfloat16):
    entries = jax.random.normal(stream_key, dims, jnp.float32) * deviation
    return jnp.minimum(jnp.maximum(entries, -reach), reach).astype(held_as)


def setup_inputs(seed: int = 0) -> dict:
    streams_of = jax.random.split(jax.random.key(seed), 3)
    return {
        "soil_heat_field": draw_soil_heat_field(jax.random.fold_in(streams_of[2], 71), 0),
        "seed_subspace": normal_values(streams_of[1], (ENSEMBLE_MEMBERS, RANK), 1.0, 6.0, jnp.float32),
    }


def gram_of(array_operand):
    return lax.dot_general(array_operand.astype(jnp.float32), array_operand.astype(jnp.float32), (((0,), (0,)), ((), ())), precision=lax.Precision.HIGHEST, preferred_element_type=jnp.float32)

def orthonormal(gram, seed_subspace):
    basis_block = seed_subspace
    for step_index in range(ITERS):
        imaged = jnp.dot(gram.astype(jnp.float32), basis_block.astype(jnp.float32), precision=lax.Precision.HIGHEST, preferred_element_type=jnp.float32)
        cholesky_lower = jnp.linalg.cholesky(gram_of(imaged))
        basis_block = lax.linalg.triangular_solve(cholesky_lower, imaged, left_side=False, lower=True, transpose_a=True)
    return basis_block

def reference(soil_heat_field, seed_subspace):
    flattened_mode_array = soil_heat_field.reshape(-1, ENSEMBLE_MEMBERS)
    gram = gram_of(flattened_mode_array) / (CELLS * SNAPS)
    triangle = jnp.linalg.cholesky(gram).T
    mode_factor = orthonormal(gram, seed_subspace)
    core_tensor = jnp.dot(flattened_mode_array.astype(jnp.float32), mode_factor.astype(jnp.float32), precision=lax.Precision.HIGHEST, preferred_element_type=jnp.float32)
    return (core_tensor.reshape(CELLS, SNAPS, RANK), mode_factor, triangle)
```

```python
import jax
import jax.numpy as jnp
from jax import lax
from jax.experimental import pallas as pl
from jax.experimental.pallas import tpu as pltpu
from jax.sharding import Mesh, PartitionSpec as P

ITERS = 3
HIGHEST = lax.Precision.HIGHEST
NB = 4
W = 128
PAIRS = [(k, l) for k in range(NB) for l in range(k, NB)]
VMEM_LIMIT = 56 * 1024 * 1024


def split(x):
    high = x.astype(jnp.bfloat16)
    return high, (x - high.astype(jnp.float32)).astype(jnp.bfloat16)


def contract(a, b, dims):
    return lax.dot_general(a, b, (dims, ((), ())), preferred_element_type=jnp.float32)


def gram_kernel(scale, x_ref, out_ref, hh, hl):
    step = pl.program_id(0)
    rows = jnp.concatenate([x_ref[k] for k in range(NB)], axis=1)
    high, low = split(rows)
    left = high.T
    part_hh = contract(left, high, ((1,), (0,)))
    part_hl = contract(left, low, ((1,), (0,)))

    @pl.when(step == 0)
    def _():
        hh[...] = part_hh
        hl[...] = part_hl

    @pl.when(step > 0)
    def _():
        hh[...] += part_hh
        hl[...] += part_hl

    @pl.when(step == pl.num_programs(0) - 1)
    def _():
        for n, (k, l) in enumerate(PAIRS):
            ks, ls = slice(W * k, W * k + W), slice(W * l, W * l + W)
            out_ref[n] = (hh[ks, ls] + (hl[ks, ls] + hl[ls, ks].T)) * scale


def gram_blocks(blocks, scale):
    rows = blocks.shape[1]
    step = 512
    return pl.pallas_call(
        lambda *refs: gram_kernel(scale, *refs),
        grid=(rows // step,),
        in_specs=[pl.BlockSpec((NB, step, W), lambda i: (0, i, 0))],
        out_specs=pl.BlockSpec((len(PAIRS), W, W), lambda i: (0, 0, 0)),
        out_shape=jax.ShapeDtypeStruct((len(PAIRS), W, W), jnp.float32),
        scratch_shapes=[pltpu.VMEM((NB * W, NB * W), jnp.float32)] * 2,
        compiler_params=pltpu.CompilerParams(vmem_limit_bytes=VMEM_LIMIT),
        cost_estimate=pl.CostEstimate(
            flops=4 * rows * (NB * W) ** 2, bytes_accessed=4 * rows * NB * W, transcendentals=0
        ),
        name="gram_blocks",
    )(blocks)


def reciprocal(d):
    r = pl.reciprocal(d, approx=True)
    r = r * (2.0 - d * r)
    return r * (2.0 - d * r)


def lanes(x, l):
    return jnp.broadcast_to(x[:, l : l + 1], (8, W))


def sublanes(x, i):
    return jnp.broadcast_to(x[i : i + 1, :], (8, W))


def factor(panels):
    count = len(panels)
    left = list(panels)
    sub = lax.broadcasted_iota(jnp.int32, (8, W), 0)
    lane = lax.broadcasted_iota(jnp.int32, (8, W), 1)
    right = [jnp.where(lane == sub + 8 * p, 1.0, 0.0).astype(jnp.float32) for p in range(count)]
    upper, inverse = [], []
    for p in range(count):
        rows0, rows1 = left[p], right[p]
        col = [lanes(rows0, 8 * p + j) for j in range(8)]
        s = {(i, j): sublanes(col[j], i) for j in range(8) for i in range(j, 8)}
        later = range(p + 1, count)
        cols = {q: [lanes(left[q], 8 * p + j) for j in range(8)] for q in later}
        for j in range(8):
            r = reciprocal(s[j, j])
            m = {i: s[i, j] * r for i in range(j + 1, 8)}
            for k in range(j + 1, 8):
                for i in range(k, 8):
                    s[i, k] = s[i, k] - m[i] * s[k, j]
            mine = jnp.where(sub > j, col[j] * r, 0.0)
            row0, row1 = sublanes(rows0, j), sublanes(rows1, j)
            for k in range(j + 1, 8):
                col[k] = col[k] - mine * s[k, j]
            rows0 = rows0 - mine * row0
            rows1 = rows1 - mine * row1
            for q in later:
                theirs = cols[q][j] * r
                for k in range(j + 1, 8):
                    cols[q][k] = cols[q][k] - theirs * s[k, j]
                left[q] = left[q] - theirs * row0
                right[q] = right[q] - theirs * row1
        pivots = s[0, 0]
        for i in range(1, 8):
            pivots = jnp.where(sub == i, s[i, i], pivots)
        scale = lax.rsqrt(pivots)
        upper.append(jnp.where(lane >= sub + 8 * p, rows0 * scale, 0.0))
        inverse.append(rows1 * scale)
    return upper, inverse


def panels_of(matrix):
    return [matrix[8 * p : 8 * p + 8, :] for p in range(matrix.shape[0] // 8)]


def exact(a, b, dims=((1,), (0,))):
    return lax.dot_general(
        a, b, (dims, ((), ())), precision=HIGHEST, preferred_element_type=jnp.float32
    )


def orthonormal_kernel(g_ref, seed_ref, basis_ref, mode_ref, gram):
    for n, (k, l) in enumerate(PAIRS):
        block = g_ref[n]
        gram[W * k : W * k + W, W * l : W * l + W] = block
        if k != l:
            gram[W * l : W * l + W, W * k : W * k + W] = block.T
    basis_ref[...] = seed_ref[...]

    def step(_, carry):
        imaged = exact(basis_ref[...], gram[...])
        small = exact(imaged, imaged, ((1,), (1,)))
        _, inverse = factor(panels_of(small))
        basis_ref[...] = exact(jnp.concatenate(inverse, axis=0), imaged)
        return carry

    lax.fori_loop(0, ITERS, step, 0)
    mode_ref[...] = basis_ref[...].T


def orthonormal(gram, seed_rows):
    size = NB * W
    return pl.pallas_call(
        orthonormal_kernel,
        out_shape=[
            jax.ShapeDtypeStruct(seed_rows.shape, jnp.float32),
            jax.ShapeDtypeStruct(seed_rows.shape[::-1], jnp.float32),
        ],
        scratch_shapes=[pltpu.VMEM((size, size), jnp.float32)],
        compiler_params=pltpu.CompilerParams(vmem_limit_bytes=VMEM_LIMIT),
        cost_estimate=pl.CostEstimate(
            flops=40_000_000_000, bytes_accessed=4 * size * size, transcendentals=0
        ),
        name="orthonormal",
    )(gram, seed_rows)


def triangle_kernel(g_ref, out_ref, rest):
    out_ref[...] = jnp.zeros_like(out_ref)
    for n, (k, l) in enumerate(PAIRS):
        rest[W * k : W * k + W, W * l : W * l + W] = g_ref[n]

    def step(b, carry):
        start = pl.multiple_of(b * W, W)
        own = pl.ds(start, W)
        upper, inverse = factor([rest[pl.ds(start + 8 * p, 8), own] for p in range(W // 8)])
        inverse = jnp.concatenate(inverse, axis=0)

        @pl.when(b < NB - 1)
        def _():
            keep = lax.broadcasted_iota(jnp.int32, (W, NB * W), 1) >= (b + 1) * W
            row = jnp.where(keep, exact(inverse, rest[own, :]), 0.0)
            out_ref[own, :] = row

            def down(c, carry):
                at = pl.ds(pl.multiple_of(c * W, W), W)
                rest[at, :] -= exact(out_ref[own, at].T, out_ref[own, :])
                return carry

            lax.fori_loop(b + 1, NB, down, 0)

        out_ref[own, own] = jnp.concatenate(upper, axis=0)
        return carry

    lax.fori_loop(0, NB, step, 0)


def triangle_of(gram):
    size = NB * W
    return pl.pallas_call(
        triangle_kernel,
        out_shape=jax.ShapeDtypeStruct((size, size), jnp.float32),
        scratch_shapes=[pltpu.VMEM((size, size), jnp.float32)],
        compiler_params=pltpu.CompilerParams(vmem_limit_bytes=VMEM_LIMIT),
        cost_estimate=pl.CostEstimate(
            flops=40_000_000_000, bytes_accessed=8 * size * size, transcendentals=0
        ),
        name="triangle",
    )(gram)


def core_kernel(basis_ref, x_ref, out_ref):
    rows = jnp.concatenate([x_ref[k, 0] for k in range(NB)], axis=1)
    high, low = split(rows)
    basis_high, basis_low = split(basis_ref[...])
    dims = ((1,), (1,))
    core = contract(basis_high, high, dims) + (
        contract(basis_high, low, dims) + contract(basis_low, high, dims)
    )
    part = core.shape[0] // NB
    for j in range(NB):
        out_ref[j, 0] = core[part * j : part * j + part, :]


def core_parts(basis, blocks):
    _, cells, snaps, _ = blocks.shape
    part = basis.shape[0] // NB
    return pl.pallas_call(
        core_kernel,
        grid=(cells,),
        in_specs=[
            pl.BlockSpec(basis.shape, lambda i: (0, 0)),
            pl.BlockSpec((NB, 1, snaps, W), lambda i: (0, i, 0, 0)),
        ],
        out_specs=pl.BlockSpec((NB, 1, part, snaps), lambda i: (0, i, 0, 0)),
        out_shape=jax.ShapeDtypeStruct((NB, cells, part, snaps), jnp.float32),
        compiler_params=pltpu.CompilerParams(vmem_limit_bytes=VMEM_LIMIT),
        cost_estimate=pl.CostEstimate(
            flops=6 * cells * snaps * NB * W * W,
            bytes_accessed=5 * cells * snaps * NB * W,
            transcendentals=0,
        ),
        name="core_parts",
    )(basis, blocks)


def exchanged(block, axis, bits):
    count = lax.axis_size(axis)
    return lax.ppermute(block, axis, [(i, i ^ bits) for i in range(count)])


def summed_over_devices(part):
    half = part.shape[0] // 2
    core = lax.axis_index("core")
    keep = lax.dynamic_slice_in_dim(part, core * half, half, 0)
    send = lax.dynamic_slice_in_dim(part, (1 - core) * half, half, 0)
    own = keep + exchanged(send, "core", 1)
    shares = lax.all_to_all(
        own.reshape(NB, half // NB, W), "x", split_axis=0, concat_axis=0, tiled=True
    )
    own = (shares[0] + shares[1]) + (shares[2] + shares[3])
    two, one, three = (exchanged(own, "y", bits) for bits in (2, 1, 3))
    own = (own + one) + (two + three)
    for bits in (1, 2, 4):
        own = own + exchanged(own, "z", bits)
    copies = jnp.broadcast_to(own[None], (NB, *own.shape))
    whole = lax.all_to_all(copies, "x", split_axis=0, concat_axis=0, tiled=True)
    whole = whole.reshape(half, W)
    return lax.all_gather(whole, "core", axis=0, tiled=True)


def to_owners(parts):
    me = lax.axis_index("x")
    arrived = [lax.dynamic_index_in_dim(parts, me, 0, keepdims=False)]
    sent = {
        bits: exchanged(
            lax.dynamic_index_in_dim(parts, me ^ bits, 0, keepdims=False), "x", bits
        )
        for bits in (2, 1, 3)
    }
    arrived += [sent[bits] for bits in (1, 2, 3)]
    low, high = (me & 1) == 1, (me & 2) == 2
    a, b, c, d = arrived
    a, b = jnp.where(low, b, a), jnp.where(low, a, b)
    c, d = jnp.where(low, d, c), jnp.where(low, c, d)
    a, c = jnp.where(high, c, a), jnp.where(high, a, c)
    b, d = jnp.where(high, d, b), jnp.where(high, b, d)
    return jnp.stack([a, b, c, d])


def local(soil_heat_field, seed_subspace):
    cells, snaps, width = soil_heat_field.shape
    devices = lax.axis_size(("x", "y", "z", "core"))
    blocks = lax.all_to_all(soil_heat_field, "x", split_axis=0, concat_axis=0, tiled=True)
    blocks = blocks.reshape(NB, cells // NB * snaps, width)
    total_rows = blocks.shape[1] * devices
    own_gram = gram_blocks(blocks, 1.0 / total_rows)
    gram = summed_over_devices(own_gram.reshape(-1, W)).reshape(own_gram.shape)
    basis, mode_factor = orthonormal(gram, seed_subspace.T)
    parts = core_parts(basis, blocks.reshape(NB, cells // NB, snaps, width))
    core_tensor = to_owners(parts)
    triangle = triangle_of(gram)
    core_tensor = core_tensor.reshape(cells, -1, snaps).transpose(0, 2, 1)
    return (core_tensor, mode_factor, triangle)


def solution(mesh):
    fine = Mesh(mesh.devices.reshape(4, -1, 8, 2), ("x", "y", "z", "core"))
    cell = ("y", "z", "core")
    return jax.shard_map(
        local,
        mesh=fine,
        in_specs=(P(cell, None, "x"), P()),
        out_specs=(P(cell, None, "x"), P(), P()),
        check_vma=False,
    )
```

```python
import jax
import jax.numpy as jnp
from jax import lax
from jax.experimental import pallas as pl
from jax.experimental.pallas import tpu as pltpu
from jax.sharding import Mesh, PartitionSpec as P

ITERS = 3
HIGHEST = lax.Precision.HIGHEST
NB = 4
W = 128
PAIRS = [(k, l) for k in range(NB) for l in range(k, NB)]
COUNTS = (3, 3, 2)
VMEM_LIMIT = 14 * 1024 * 1024


def split(x):
    high = x.astype(jnp.bfloat16)
    return high, (x - high.astype(jnp.float32)).astype(jnp.bfloat16)


def contract(a, b, dims):
    return lax.dot_general(a, b, (dims, ((), ())), preferred_element_type=jnp.float32)


def gram_kernel(scale, first, me_ref, *refs):
    pieces, refs = refs[:NB], refs[NB:]
    before, (out_ref, high_ref, low_ref, rows) = refs[:-4], refs[-4:]
    me = me_ref[0]
    for b, piece in enumerate(pieces):
        place = pl.multiple_of((me ^ b) * W, W)
        rows[:, pl.ds(place, W)] = piece[...].reshape(rows.shape[0], W)
    high, low = split(rows[...])
    high_ref[...] = high
    low_ref[...] = low
    left = high.T
    hh = contract(left, high, ((1,), (0,)))
    hl = contract(left, low, ((1,), (0,)))
    for n, (k, l) in enumerate(PAIRS):
        ks, ls = slice(W * k, W * k + W), slice(W * l, W * l + W)
        part = (hh[ks, ls] + (hl[ks, ls] + hl[ls, ks].T)) * scale
        out_ref[n] = part if first else before[0][n] + part


def gram_chunk(me, field, start, cells, arrived, before, scale):
    snaps = field.shape[2]
    rows = cells * snaps
    gram = jax.ShapeDtypeStruct((len(PAIRS), W, W), jnp.float32)
    halves = jax.ShapeDtypeStruct((rows, NB * W), jnp.bfloat16)
    whole = lambda shape: pl.BlockSpec(shape, lambda i, me: (0,) * len(shape))
    own = pl.BlockSpec(
        (pl.Squeezed(), pl.Element(cells), pl.Element(snaps), pl.Element(W)),
        lambda i, me: (me[0], start, 0, 0),
    )
    return pl.pallas_call(
        lambda *refs: gram_kernel(scale, before is None, *refs),
        grid_spec=pltpu.PrefetchScalarGridSpec(
            num_scalar_prefetch=1,
            grid=(1,),
            in_specs=[own]
            + [whole((cells, snaps, W))] * (NB - 1)
            + ([] if before is None else [whole(gram.shape)]),
            out_specs=[whole(gram.shape), whole(halves.shape), whole(halves.shape)],
            scratch_shapes=[pltpu.VMEM((rows, NB * W), jnp.float32)],
        ),
        out_shape=[gram, halves, halves],
        compiler_params=pltpu.CompilerParams(vmem_limit_bytes=VMEM_LIMIT),
        cost_estimate=pl.CostEstimate(
            flops=4 * rows * (NB * W) ** 2, bytes_accessed=8 * rows * NB * W, transcendentals=0
        ),
        name="gram_chunk",
    )(me, field, *arrived, *([] if before is None else [before]))


def reciprocal(d):
    r = pltpu.reciprocal(d, approx=True)
    return r * (2.0 - d * r)


def lanes(x, l):
    return jnp.broadcast_to(x[:, l : l + 1], (8, W))


def sublanes(x, i):
    return jnp.broadcast_to(x[i : i + 1, :], (8, W))


def factor(panels):
    count = len(panels)
    left = list(panels)
    sub = lax.broadcasted_iota(jnp.int32, (8, W), 0)
    lane = lax.broadcasted_iota(jnp.int32, (8, W), 1)
    right = [jnp.where(lane == sub + 8 * p, 1.0, 0.0).astype(jnp.float32) for p in range(count)]
    upper, inverse = [], []
    for p in range(count):
        rows0, rows1 = left[p], right[p]
        col = [lanes(rows0, 8 * p + j) for j in range(8)]
        s = {(i, j): sublanes(col[j], i) for j in range(8) for i in range(j, 8)}
        later = range(p + 1, count)
        cols = {q: [lanes(left[q], 8 * p + j) for j in range(8)] for q in later}
        for j in range(8):
            r = reciprocal(s[j, j])
            m = {i: s[i, j] * r for i in range(j + 1, 8)}
            for k in range(j + 1, 8):
                for i in range(k, 8):
                    s[i, k] = s[i, k] - m[i] * s[k, j]
            mine = jnp.where(sub > j, col[j] * r, 0.0)
            row0, row1 = sublanes(rows0, j), sublanes(rows1, j)
            for k in range(j + 1, 8):
                col[k] = col[k] - mine * s[k, j]
            rows0 = rows0 - mine * row0
            rows1 = rows1 - mine * row1
            for q in later:
                theirs = cols[q][j] * r
                for k in range(j + 1, 8):
                    cols[q][k] = cols[q][k] - theirs * s[k, j]
                left[q] = left[q] - theirs * row0
                right[q] = right[q] - theirs * row1
        pivots = s[0, 0]
        for i in range(1, 8):
            pivots = jnp.where(sub == i, s[i, i], pivots)
        scale = lax.rsqrt(pivots)
        upper.append(jnp.where(lane >= sub + 8 * p, rows0 * scale, 0.0))
        inverse.append(rows1 * scale)
    return upper, inverse


def panels_of(matrix):
    return [matrix[8 * p : 8 * p + 8, :] for p in range(matrix.shape[0] // 8)]


def exact(a, b, dims=((1,), (0,))):
    return lax.dot_general(
        a, b, (dims, ((), ())), precision=HIGHEST, preferred_element_type=jnp.float32
    )


def orthonormal_steps(g_ref, seed_ref, basis_ref, gram):
    for n, (k, l) in enumerate(PAIRS):
        block = g_ref[n]
        gram[W * k : W * k + W, W * l : W * l + W] = block
        if k != l:
            gram[W * l : W * l + W, W * k : W * k + W] = block.T
    basis_ref[...] = seed_ref[...]

    def step(_, carry):
        imaged = exact(basis_ref[...], gram[...])
        small = exact(imaged, imaged, ((1,), (1,)))
        _, inverse = factor(panels_of(small))
        basis_ref[...] = exact(jnp.concatenate(inverse, axis=0), imaged)
        return carry

    lax.fori_loop(0, ITERS, step, 0)


def triangle_steps(g_ref, out_ref, rest):
    out_ref[...] = jnp.zeros_like(out_ref)
    for n, (k, l) in enumerate(PAIRS):
        rest[W * k : W * k + W, W * l : W * l + W] = g_ref[n]

    def step(b, carry):
        start = pl.multiple_of(b * W, W)
        own = pl.ds(start, W)
        upper, inverse = factor([rest[pl.ds(start + 8 * p, 8), own] for p in range(W // 8)])
        inverse = jnp.concatenate(inverse, axis=0)

        @pl.when(b < NB - 1)
        def _():
            keep = lax.broadcasted_iota(jnp.int32, (W, NB * W), 1) >= (b + 1) * W
            row = jnp.where(keep, exact(inverse, rest[own, :]), 0.0)
            out_ref[own, :] = row

            def down(c, carry):
                at = pl.ds(pl.multiple_of(c * W, W), W)
                rest[at, :] -= exact(out_ref[own, at].T, out_ref[own, :])
                return carry

            lax.fori_loop(b + 1, NB, down, 0)

        out_ref[own, own] = jnp.concatenate(upper, axis=0)
        return carry

    lax.fori_loop(0, NB, step, 0)


def either_kernel(core_ref, g_ref, seed_ref, basis_ref, triangle_ref, gram):
    @pl.when(core_ref[0] == 0)
    def _():
        orthonormal_steps(g_ref, seed_ref, basis_ref, gram)

    @pl.when(core_ref[0] != 0)
    def _():
        triangle_steps(g_ref, triangle_ref, gram)


def basis_or_triangle(core, gram, seed_rows):
    size = NB * W
    vmem = pl.BlockSpec(memory_space=pltpu.VMEM)
    return pl.pallas_call(
        either_kernel,
        in_specs=[pl.BlockSpec(memory_space=pltpu.SMEM), vmem, vmem],
        out_specs=[vmem, vmem],
        out_shape=[
            jax.ShapeDtypeStruct(seed_rows.shape, jnp.float32),
            jax.ShapeDtypeStruct((size, size), jnp.float32),
        ],
        scratch_shapes=[pltpu.VMEM((size, size), jnp.float32)],
        compiler_params=pltpu.CompilerParams(vmem_limit_bytes=VMEM_LIMIT),
        cost_estimate=pl.CostEstimate(
            flops=40_000_000_000, bytes_accessed=8 * size * size, transcendentals=0
        ),
        name="basis_or_triangle",
    )(core, gram, seed_rows)


def core_kernel(counts, snaps, me_ref, own_ref, other_ref, *refs):
    halves, (mode_ref, *outs), basis = refs[: 2 * len(counts)], refs[2 * len(counts) : -1], refs[-1]
    me, part = me_ref[0], own_ref.shape[0] // NB
    basis[...] = jnp.where(me_ref[1] == 0, own_ref[...], other_ref[...])
    mode_ref[...] = basis[...].T
    turned = [basis[pl.ds(pl.multiple_of((me ^ b) * part, part), part), :] for b in range(NB)]
    high, low = split(jnp.concatenate(turned, axis=0).T)
    weights = jnp.concatenate([high, low], axis=1)
    cell = 0
    for c, count in enumerate(counts):
        high_ref, low_ref = halves[2 * c : 2 * c + 2]
        for i in range(count):
            rows = slice(snaps * i, snaps * i + snaps)
            both = contract(high_ref[rows, :], weights, ((1,), (0,)))
            more = contract(low_ref[rows, :], high, ((1,), (0,)))
            core = (both[:, :W] + (both[:, W:] + more)).T
            for b in range(NB):
                outs[b][cell] = core[part * b : part * b + part, :]
            cell += 1


def core_parts(place, own_basis, other_basis, halves, counts, snaps):
    rank, size = own_basis.shape
    cells = sum(counts)
    operands = [half for pair in halves for half in pair]
    vmem = pl.BlockSpec(memory_space=pltpu.VMEM)
    return pl.pallas_call(
        lambda *refs: core_kernel(counts, snaps, *refs),
        in_specs=[pl.BlockSpec(memory_space=pltpu.SMEM)] + [vmem] * (2 + len(operands)),
        out_specs=[vmem] * (1 + NB),
        out_shape=[jax.ShapeDtypeStruct((size, rank), jnp.float32)]
        + [jax.ShapeDtypeStruct((cells, rank // NB, snaps), jnp.float32)] * NB,
        scratch_shapes=[pltpu.VMEM((rank, size), jnp.float32)],
        compiler_params=pltpu.CompilerParams(vmem_limit_bytes=VMEM_LIMIT),
        cost_estimate=pl.CostEstimate(
            flops=6 * cells * snaps * size * rank,
            bytes_accessed=5 * cells * snaps * size,
            transcendentals=0,
        ),
        name="core_parts",
    )(place, own_basis, other_basis, *operands)


def placed_kernel(me_ref, *refs):
    parts, (out_ref, sems) = refs[:NB], refs[NB:]
    copies = [
        pltpu.make_async_copy(part, out_ref.at[me_ref[0] ^ b], sems.at[b])
        for b, part in enumerate(parts)
    ]
    for copy in copies:
        copy.start()
    for copy in copies:
        copy.wait()


def placed(me, parts):
    anywhere = pl.BlockSpec(memory_space=pl.ANY)
    return pl.pallas_call(
        placed_kernel,
        in_specs=[pl.BlockSpec(memory_space=pltpu.SMEM)] + [anywhere] * NB,
        out_specs=anywhere,
        out_shape=jax.ShapeDtypeStruct((NB, *parts[0].shape), jnp.float32),
        scratch_shapes=[pltpu.SemaphoreType.DMA((NB,))],
        name="placed",
    )(me, *parts)


def exchanged(block, axis, bits):
    count = lax.axis_size(axis)
    return lax.ppermute(block, axis, [(i, i ^ bits) for i in range(count)])


def summed_over_devices(part):
    axes = ("x", "core")
    count = lax.axis_size(axes)
    shares = lax.all_to_all(
        part.reshape(count, -1, W), axes, split_axis=0, concat_axis=0, tiled=True
    )
    own = shares.sum(axis=0)
    two, one, three = (exchanged(own, "y", bits) for bits in (2, 1, 3))
    own = (own + one) + (two + three)
    for bits in (1, 2, 4):
        own = own + exchanged(own, "z", bits)
    copies = jnp.broadcast_to(own[None], (count, *own.shape))
    whole = lax.all_to_all(copies, axes, split_axis=0, concat_axis=0, tiled=True)
    return whole.reshape(-1, W)


def local(soil_heat_field, seed_subspace):
    cells, snaps, width = soil_heat_field.shape
    devices = lax.axis_size(("x", "y", "z", "core"))
    me, core = lax.axis_index("x"), lax.axis_index("core")
    place = jnp.stack([me, core]).astype(jnp.int32)
    field = soil_heat_field.reshape(NB, cells // NB, snaps, width)
    scale = 1.0 / (cells // NB * snaps * devices)
    counts = COUNTS

    gram, halves, start = None, [], 0
    arrived = []
    for count in counts:
        got = {}
        for bits in (2, 1, 3):
            send = lax.dynamic_slice(
                field, (me ^ bits, start, 0, 0), (1, count, snaps, width)
            )[0]
            got[bits] = exchanged(send, "x", bits)
        arrived.append([got[bits] for bits in (1, 2, 3)])
        start += count
    start = 0
    for count, others in zip(counts, arrived):
        gram, high, low = gram_chunk(place, field, start, count, others, gram, scale)
        halves.append((high, low))
        start += count

    gram = summed_over_devices(gram.reshape(-1, W)).reshape(gram.shape)
    basis, triangle = basis_or_triangle(place[1:], gram, seed_subspace.T)
    other_basis = exchanged(basis, "core", 1)
    triangle, other_basis = lax.optimization_barrier((triangle, other_basis))
    other_triangle = exchanged(triangle, "core", 1)
    mode_factor, *parts = core_parts(place, basis, other_basis, halves, counts, snaps)
    sent = {bits: exchanged(parts[bits], "x", bits) for bits in (2, 1, 3)}
    triangle = jnp.where(core == 0, other_triangle, triangle)
    core_tensor = placed(place, [parts[0]] + [sent[bits] for bits in (1, 2, 3)])
    core_tensor = core_tensor.reshape(cells, -1, snaps).transpose(0, 2, 1)
    return (core_tensor, mode_factor, triangle)


def solution(mesh):
    fine = Mesh(mesh.devices.reshape(4, -1, 8, 2), ("x", "y", "z", "core"))
    cell = ("y", "z", "core")
    return jax.shard_map(
        local,
        mesh=fine,
        in_specs=(P(cell, None, "x"), P()),
        out_specs=(P(cell, None, "x"), P(), P()),
        check_vma=False,
    )
```

```python
import jax
import jax.numpy as jnp
from jax import lax
from jax.experimental import pallas as pl
from jax.experimental.pallas import tpu as pltpu
from jax.sharding import Mesh, PartitionSpec as P

ITERS = 3
HIGHEST = lax.Precision.HIGHEST
NB = 4
W = 128
PAIRS = [(k, l) for k in range(NB) for l in range(k, NB)]
COUNTS = (3, 3, 2)
VMEM_LIMIT = 60 * 1024 * 1024


def split(x):
    high = x.astype(jnp.bfloat16)
    return high, (x - high.astype(jnp.float32)).astype(jnp.bfloat16)


def contract(a, b, dims):
    return lax.dot_general(a, b, (dims, ((), ())), preferred_element_type=jnp.float32)


def gram_kernel(scale, start, me_ref, field, *refs):
    others, refs = refs[: NB - 1], refs[NB - 1 :]
    before, (out_ref, high_ref, low_ref, rows, high, low, total, sems) = refs[:-8], refs[-8:]
    cells, snaps, size = rows.shape
    me = me_ref[0]
    copies = []
    for b, piece in enumerate((field.at[me, pl.ds(start, cells)], *others)):
        place = pl.multiple_of((me ^ b) * W, W)
        copies.append(pltpu.make_async_copy(piece, rows.at[:, :, pl.ds(place, W)], sems.at[b]))
    if before:
        copies.append(pltpu.make_async_copy(before[0], total, sems.at[NB]))
    for copy in copies:
        copy.start()
    for copy in copies:
        copy.wait()
    high[...], low[...] = split(rows[...].reshape(cells * snaps, size))
    halves = [
        pltpu.make_async_copy(high, high_ref, sems.at[NB + 1]),
        pltpu.make_async_copy(low, low_ref, sems.at[NB + 2]),
    ]
    for copy in halves:
        copy.start()
    left = high[...].T
    hh = contract(left, high[...], ((1,), (0,)))
    hl = contract(left, low[...], ((1,), (0,)))
    for n, (k, l) in enumerate(PAIRS):
        ks, ls = slice(W * k, W * k + W), slice(W * l, W * l + W)
        part = (hh[ks, ls] + (hl[ks, ls] + hl[ls, ks].T)) * scale
        total[n] = total[n] + part if before else part
    result = pltpu.make_async_copy(total, out_ref, sems.at[NB + 3])
    result.start()
    for copy in (*halves, result):
        copy.wait()


def gram_chunk(me, field, start, cells, arrived, before, scale):
    snaps = field.shape[2]
    rows = cells * snaps
    gram = (len(PAIRS), W, W)
    halves = jax.ShapeDtypeStruct((rows, NB * W), jnp.bfloat16)
    anywhere = pl.BlockSpec(memory_space=pl.ANY)
    operands = [field, *arrived] + ([] if before is None else [before])
    return pl.pallas_call(
        lambda *refs: gram_kernel(scale, start, *refs),
        in_specs=[pl.BlockSpec(memory_space=pltpu.SMEM)] + [anywhere] * len(operands),
        out_specs=[anywhere] * 3,
        out_shape=[jax.ShapeDtypeStruct(gram, jnp.float32), halves, halves],
        scratch_shapes=[
            pltpu.VMEM((cells, snaps, NB * W), jnp.float32),
            pltpu.VMEM(halves.shape, jnp.bfloat16),
            pltpu.VMEM(halves.shape, jnp.bfloat16),
            pltpu.VMEM(gram, jnp.float32),
            pltpu.SemaphoreType.DMA((NB + 4,)),
        ],
        compiler_params=pltpu.CompilerParams(vmem_limit_bytes=VMEM_LIMIT),
        cost_estimate=pl.CostEstimate(
            flops=4 * rows * (NB * W) ** 2, bytes_accessed=8 * rows * NB * W, transcendentals=0
        ),
        name="gram_chunk",
    )(me, *operands)


def reciprocal(d):
    r = pltpu.reciprocal(d, approx=True)
    return r * (2.0 - d * r)


def lanes(x, l):
    return jnp.broadcast_to(x[:, l : l + 1], (8, W))


def sublanes(x, i):
    return jnp.broadcast_to(x[i : i + 1, :], (8, W))


def factor(panels):
    count = len(panels)
    left = list(panels)
    sub = lax.broadcasted_iota(jnp.int32, (8, W), 0)
    lane = lax.broadcasted_iota(jnp.int32, (8, W), 1)
    right = [jnp.where(lane == sub + 8 * p, 1.0, 0.0).astype(jnp.float32) for p in range(count)]
    upper, inverse = [], []
    for p in range(count):
        rows0, rows1 = left[p], right[p]
        col = [lanes(rows0, 8 * p + j) for j in range(8)]
        s = {(i, j): sublanes(col[j], i) for j in range(8) for i in range(j, 8)}
        later = range(p + 1, count)
        cols = {q: [lanes(left[q], 8 * p + j) for j in range(8)] for q in later}
        for j in range(8):
            r = reciprocal(s[j, j])
            m = {i: s[i, j] * r for i in range(j + 1, 8)}
            for k in range(j + 1, 8):
                for i in range(k, 8):
                    s[i, k] = s[i, k] - m[i] * s[k, j]
            mine = jnp.where(sub > j, col[j] * r, 0.0)
            row0, row1 = sublanes(rows0, j), sublanes(rows1, j)
            for k in range(j + 1, 8):
                col[k] = col[k] - mine * s[k, j]
            rows0 = rows0 - mine * row0
            rows1 = rows1 - mine * row1
            for q in later:
                theirs = cols[q][j] * r
                for k in range(j + 1, 8):
                    cols[q][k] = cols[q][k] - theirs * s[k, j]
                left[q] = left[q] - theirs * row0
                right[q] = right[q] - theirs * row1
        pivots = s[0, 0]
        for i in range(1, 8):
            pivots = jnp.where(sub == i, s[i, i], pivots)
        scale = lax.rsqrt(pivots)
        upper.append(jnp.where(lane >= sub + 8 * p, rows0 * scale, 0.0))
        inverse.append(rows1 * scale)
    return upper, inverse


def panels_of(matrix):
    return [matrix[8 * p : 8 * p + 8, :] for p in range(matrix.shape[0] // 8)]


def exact(a, b, dims=((1,), (0,))):
    return lax.dot_general(
        a, b, (dims, ((), ())), precision=HIGHEST, preferred_element_type=jnp.float32
    )


def orthonormal_steps(g_ref, seed_ref, basis_ref, gram):
    for n, (k, l) in enumerate(PAIRS):
        block = g_ref[n]
        gram[W * k : W * k + W, W * l : W * l + W] = block
        if k != l:
            gram[W * l : W * l + W, W * k : W * k + W] = block.T
    basis_ref[...] = seed_ref[...].T

    def step(_, carry):
        imaged = exact(basis_ref[...], gram[...])
        small = exact(imaged, imaged, ((1,), (1,)))
        _, inverse = factor(panels_of(small))
        basis_ref[...] = exact(jnp.concatenate(inverse, axis=0), imaged)
        return carry

    lax.fori_loop(0, ITERS, step, 0)


def triangle_steps(g_ref, out_ref, rest):
    out_ref[...] = jnp.zeros_like(out_ref)
    for n, (k, l) in enumerate(PAIRS):
        rest[W * k : W * k + W, W * l : W * l + W] = g_ref[n]

    def step(b, carry):
        start = pl.multiple_of(b * W, W)
        own = pl.ds(start, W)
        upper, inverse = factor([rest[pl.ds(start + 8 * p, 8), own] for p in range(W // 8)])
        inverse = jnp.concatenate(inverse, axis=0)

        @pl.when(b < NB - 1)
        def _():
            keep = lax.broadcasted_iota(jnp.int32, (W, NB * W), 1) >= (b + 1) * W
            row = jnp.where(keep, exact(inverse, rest[own, :]), 0.0)
            out_ref[own, :] = row

            def down(c, carry):
                at = pl.ds(pl.multiple_of(c * W, W), W)
                rest[at, :] -= exact(out_ref[own, at].T, out_ref[own, :])
                return carry

            lax.fori_loop(b + 1, NB, down, 0)

        out_ref[own, own] = jnp.concatenate(upper, axis=0)
        return carry

    lax.fori_loop(0, NB, step, 0)


def copied(*copies):
    for copy in copies:
        copy.start()
    for copy in copies:
        copy.wait()


def either_kernel(core_ref, g_ref, seed_ref, basis_ref, triangle_ref, gram, blocks, seed, basis, triangle, sems):
    copied(
        pltpu.make_async_copy(g_ref, blocks, sems.at[0]),
        pltpu.make_async_copy(seed_ref, seed, sems.at[1]),
    )

    @pl.when(core_ref[0] == 0)
    def _():
        orthonormal_steps(blocks, seed, basis, gram)
        copied(pltpu.make_async_copy(basis, basis_ref, sems.at[2]))

    @pl.when(core_ref[0] != 0)
    def _():
        triangle_steps(blocks, triangle, gram)
        copied(pltpu.make_async_copy(triangle, triangle_ref, sems.at[3]))


def basis_or_triangle(core, gram, seed):
    size = NB * W
    anywhere = pl.BlockSpec(memory_space=pl.ANY)
    return pl.pallas_call(
        either_kernel,
        in_specs=[pl.BlockSpec(memory_space=pltpu.SMEM), anywhere, anywhere],
        out_specs=[anywhere, anywhere],
        out_shape=[
            jax.ShapeDtypeStruct(seed.shape[::-1], jnp.float32),
            jax.ShapeDtypeStruct((size, size), jnp.float32),
        ],
        scratch_shapes=[
            pltpu.VMEM((size, size), jnp.float32),
            pltpu.VMEM(gram.shape, jnp.float32),
            pltpu.VMEM(seed.shape, jnp.float32),
            pltpu.VMEM(seed.shape[::-1], jnp.float32),
            pltpu.VMEM((size, size), jnp.float32),
            pltpu.SemaphoreType.DMA((4,)),
        ],
        compiler_params=pltpu.CompilerParams(vmem_limit_bytes=VMEM_LIMIT),
        cost_estimate=pl.CostEstimate(
            flops=40_000_000_000, bytes_accessed=8 * size * size, transcendentals=0
        ),
        name="basis_or_triangle",
    )(core, gram, seed)


def core_kernel(counts, snaps, me_ref, own_ref, other_ref, *refs):
    n = 2 * len(counts)
    sources, refs = refs[:n], refs[n:]
    mode_ref, *out_refs = refs[: 1 + NB]
    refs = refs[1 + NB :]
    halves, (basis, mode, parts, in_sems, out_sems) = refs[:n], refs[n:]
    me, part = me_ref[0], basis.shape[0] // NB
    arrivals = [
        pltpu.make_async_copy(source, half, in_sems.at[i])
        for i, (source, half) in enumerate(zip(sources, halves))
    ]

    @pl.when(me_ref[1] == 0)
    def _():
        copied(pltpu.make_async_copy(own_ref, basis, in_sems.at[n]))

    @pl.when(me_ref[1] != 0)
    def _():
        copied(pltpu.make_async_copy(other_ref, basis, in_sems.at[n]))

    for copy in arrivals:
        copy.start()
    mode[...] = basis[...].T
    leaving = [pltpu.make_async_copy(mode, mode_ref, out_sems.at[NB])]
    leaving[0].start()
    turned = [basis[pl.ds(pl.multiple_of((me ^ b) * part, part), part), :] for b in range(NB)]
    high, low = split(jnp.concatenate(turned, axis=0).T)
    weights = jnp.concatenate([high, low], axis=1)
    cell = 0
    for c, count in enumerate(counts):
        high_ref, low_ref = halves[2 * c : 2 * c + 2]
        arrivals[2 * c].wait()
        arrivals[2 * c + 1].wait()
        for i in range(count):
            rows = slice(snaps * i, snaps * i + snaps)
            both = contract(high_ref[rows, :], weights, ((1,), (0,)))
            more = contract(low_ref[rows, :], high, ((1,), (0,)))
            core = (both[:, :W] + (both[:, W:] + more)).T
            for b in range(NB):
                parts[b, cell] = core[part * b : part * b + part, :]
            cell += 1
    for b in range(NB):
        leaving.append(pltpu.make_async_copy(parts.at[b], out_refs[b], out_sems.at[b]))
        leaving[-1].start()
    for copy in leaving:
        copy.wait()


def core_parts(place, own_basis, other_basis, halves, counts, snaps):
    rank, size = own_basis.shape
    cells = sum(counts)
    operands = [half for pair in halves for half in pair]
    anywhere = pl.BlockSpec(memory_space=pl.ANY)
    return pl.pallas_call(
        lambda *refs: core_kernel(counts, snaps, *refs),
        in_specs=[pl.BlockSpec(memory_space=pltpu.SMEM)] + [anywhere] * (2 + len(operands)),
        out_specs=[anywhere] * (1 + NB),
        out_shape=[jax.ShapeDtypeStruct((size, rank), jnp.float32)]
        + [jax.ShapeDtypeStruct((cells, rank // NB, snaps), jnp.float32)] * NB,
        scratch_shapes=[pltpu.VMEM(half.shape, half.dtype) for half in operands]
        + [
            pltpu.VMEM((rank, size), jnp.float32),
            pltpu.VMEM((size, rank), jnp.float32),
            pltpu.VMEM((NB, cells, rank // NB, snaps), jnp.float32),
            pltpu.SemaphoreType.DMA((len(operands) + 1,)),
            pltpu.SemaphoreType.DMA((NB + 1,)),
        ],
        compiler_params=pltpu.CompilerParams(vmem_limit_bytes=VMEM_LIMIT),
        cost_estimate=pl.CostEstimate(
            flops=6 * cells * snaps * size * rank,
            bytes_accessed=5 * cells * snaps * size,
            transcendentals=0,
        ),
        name="core_parts",
    )(place, own_basis, other_basis, *operands)


def placed_kernel(me_ref, *refs):
    parts, (out_ref, held, sems) = refs[:NB], refs[NB:]
    arrivals = [
        pltpu.make_async_copy(part, held.at[b], sems.at[b]) for b, part in enumerate(parts)
    ]
    leaving = [
        pltpu.make_async_copy(held.at[b], out_ref.at[me_ref[0] ^ b], sems.at[NB + b])
        for b in range(NB)
    ]
    for copy in arrivals:
        copy.start()
    for arrival, copy in zip(arrivals, leaving):
        arrival.wait()
        copy.start()
    for copy in leaving:
        copy.wait()


def placed(me, parts):
    anywhere = pl.BlockSpec(memory_space=pl.ANY)
    return pl.pallas_call(
        placed_kernel,
        in_specs=[pl.BlockSpec(memory_space=pltpu.SMEM)] + [anywhere] * NB,
        out_specs=anywhere,
        out_shape=jax.ShapeDtypeStruct((NB, *parts[0].shape), jnp.float32),
        scratch_shapes=[
            pltpu.VMEM((NB, *parts[0].shape), jnp.float32),
            pltpu.SemaphoreType.DMA((2 * NB,)),
        ],
        compiler_params=pltpu.CompilerParams(vmem_limit_bytes=VMEM_LIMIT // 6),
        name="placed",
    )(me, *parts)


def exchanged(block, axis, bits):
    count = lax.axis_size(axis)
    return lax.ppermute(block, axis, [(i, i ^ bits) for i in range(count)])


def summed_over_devices(part):
    half = part.shape[0] // 2
    core = lax.axis_index("core")
    keep = lax.dynamic_slice_in_dim(part, core * half, half, 0)
    send = lax.dynamic_slice_in_dim(part, (1 - core) * half, half, 0)
    own = keep + exchanged(send, "core", 1)
    shares = lax.all_to_all(
        own.reshape(NB, half // NB, W), "x", split_axis=0, concat_axis=0, tiled=True
    )
    own = (shares[0] + shares[1]) + (shares[2] + shares[3])
    two, one, three = (exchanged(own, "y", bits) for bits in (2, 1, 3))
    own = (own + one) + (two + three)
    own = own + exchanged(own, "z", 1)
    four, two, six = (exchanged(own, "z", bits) for bits in (4, 2, 6))
    own = (own + two) + (four + six)
    copies = jnp.broadcast_to(own[None], (NB, *own.shape))
    whole = lax.all_to_all(copies, "x", split_axis=0, concat_axis=0, tiled=True)
    whole = whole.reshape(half, W)
    return lax.all_gather(whole, "core", axis=0, tiled=True)


def local(soil_heat_field, seed_subspace):
    cells, snaps, width = soil_heat_field.shape
    devices = lax.axis_size(("x", "y", "z", "core"))
    me, core = lax.axis_index("x"), lax.axis_index("core")
    place = jnp.stack([me, core]).astype(jnp.int32)
    field = soil_heat_field.reshape(NB, cells // NB, snaps, width)
    scale = 1.0 / (cells // NB * snaps * devices)
    counts = COUNTS

    gram, halves, start = None, [], 0
    arrived, later = [], field
    for count in counts:
        got, sends = {}, []
        for bits in (2, 1, 3):
            send = lax.dynamic_slice(
                later, (me ^ bits, start, 0, 0), (1, count, snaps, width)
            )[0]
            got[bits] = exchanged(send, "x", bits)
            sends.append(send)
        later, *_ = lax.optimization_barrier((later, *sends))
        arrived.append([got[bits] for bits in (1, 2, 3)])
        start += count
    start = 0
    for count, others in zip(counts, arrived):
        gram, high, low = gram_chunk(place, field, start, count, others, gram, scale)
        halves.append((high, low))
        start += count

    gram = summed_over_devices(gram.reshape(-1, W)).reshape(gram.shape)
    basis, triangle = basis_or_triangle(place[1:], gram, seed_subspace)
    other_basis = exchanged(basis, "core", 1)
    triangle, other_basis = lax.optimization_barrier((triangle, other_basis))
    other_triangle = exchanged(triangle, "core", 1)
    mode_factor, *parts = core_parts(place, basis, other_basis, halves, counts, snaps)
    sent = {bits: exchanged(parts[bits], "x", bits) for bits in (2, 1, 3)}
    triangle = jnp.where(core == 0, other_triangle, triangle)
    own_part, triangle = lax.optimization_barrier((parts[0], triangle))
    core_tensor = placed(place, [own_part] + [sent[bits] for bits in (1, 2, 3)])
    core_tensor = core_tensor.reshape(cells, -1, snaps).transpose(0, 2, 1)
    return (core_tensor, mode_factor, triangle)


def solution(mesh):
    fine = Mesh(mesh.devices.reshape(4, -1, 8, 2), ("x", "y", "z", "core"))
    cell = ("y", "z", "core")
    return jax.shard_map(
        local,
        mesh=fine,
        in_specs=(P(cell, None, "x"), P()),
        out_specs=(P(cell, None, "x"), P(), P()),
        check_vma=False,
    )
```

```python
import jax
import jax.numpy as jnp
from jax import lax
from jax.experimental import pallas as pl
from jax.experimental.pallas import tpu as pltpu
from jax.sharding import Mesh, PartitionSpec as P

ITERS = 3
HIGHEST = lax.Precision.HIGHEST
NB = 4
W = 128
PAIRS = [(k, l) for k in range(NB) for l in range(k, NB)]
COUNTS = (1, 3, 3, 1)
VMEM_LIMIT = 60 * 1024 * 1024


def split(x):
    high = x.astype(jnp.bfloat16)
    return high, (x - high.astype(jnp.float32)).astype(jnp.bfloat16)


def contract(a, b, dims):
    return lax.dot_general(a, b, (dims, ((), ())), preferred_element_type=jnp.float32)


def gram_kernel(scale, start, me_ref, field, *refs):
    others, refs = refs[: NB - 1], refs[NB - 1 :]
    before, (out_ref, high_ref, low_ref, rows, high, low, total, sems) = refs[:-8], refs[-8:]
    cells, snaps, size = rows.shape
    me = me_ref[0]
    copies = []
    for b, piece in enumerate((field.at[me, pl.ds(start, cells)], *others)):
        place = pl.multiple_of((me ^ b) * W, W)
        copies.append(pltpu.make_async_copy(piece, rows.at[:, :, pl.ds(place, W)], sems.at[b]))
    if before:
        copies.append(pltpu.make_async_copy(before[0], total, sems.at[NB]))
    for copy in copies:
        copy.start()
    for copy in copies:
        copy.wait()
    high[...], low[...] = split(rows[...].reshape(cells * snaps, size))
    halves = [
        pltpu.make_async_copy(high, high_ref, sems.at[NB + 1]),
        pltpu.make_async_copy(low, low_ref, sems.at[NB + 2]),
    ]
    for copy in halves:
        copy.start()
    left = high[...].T
    hh = contract(left, high[...], ((1,), (0,)))
    hl = contract(left, low[...], ((1,), (0,)))
    for n, (k, l) in enumerate(PAIRS):
        ks, ls = slice(W * k, W * k + W), slice(W * l, W * l + W)
        part = (hh[ks, ls] + (hl[ks, ls] + hl[ls, ks].T)) * scale
        total[n] = total[n] + part if before else part
    result = pltpu.make_async_copy(total, out_ref, sems.at[NB + 3])
    result.start()
    for copy in (*halves, result):
        copy.wait()


def gram_chunk(me, field, start, cells, arrived, before, scale):
    snaps = field.shape[2]
    rows = cells * snaps
    gram = (len(PAIRS), W, W)
    halves = jax.ShapeDtypeStruct((rows, NB * W), jnp.bfloat16)
    anywhere = pl.BlockSpec(memory_space=pl.ANY)
    operands = [field, *arrived] + ([] if before is None else [before])
    return pl.pallas_call(
        lambda *refs: gram_kernel(scale, start, *refs),
        in_specs=[pl.BlockSpec(memory_space=pltpu.SMEM)] + [anywhere] * len(operands),
        out_specs=[anywhere] * 3,
        out_shape=[jax.ShapeDtypeStruct(gram, jnp.float32), halves, halves],
        scratch_shapes=[
            pltpu.VMEM((cells, snaps, NB * W), jnp.float32),
            pltpu.VMEM(halves.shape, jnp.bfloat16),
            pltpu.VMEM(halves.shape, jnp.bfloat16),
            pltpu.VMEM(gram, jnp.float32),
            pltpu.SemaphoreType.DMA((NB + 4,)),
        ],
        compiler_params=pltpu.CompilerParams(vmem_limit_bytes=VMEM_LIMIT),
        cost_estimate=pl.CostEstimate(
            flops=4 * rows * (NB * W) ** 2, bytes_accessed=8 * rows * NB * W, transcendentals=0
        ),
        name="gram_chunk",
    )(me, *operands)


def reciprocal(d):
    r = pltpu.reciprocal(d, approx=True)
    return r * (2.0 - d * r)


def lanes(x, l):
    return jnp.broadcast_to(x[:, l : l + 1], (8, W))


def sublanes(x, i):
    return jnp.broadcast_to(x[i : i + 1, :], (8, W))


def factor(panels):
    count = len(panels)
    left = list(panels)
    sub = lax.broadcasted_iota(jnp.int32, (8, W), 0)
    lane = lax.broadcasted_iota(jnp.int32, (8, W), 1)
    right = [jnp.where(lane == sub + 8 * p, 1.0, 0.0).astype(jnp.float32) for p in range(count)]
    upper, inverse = [], []
    for p in range(count):
        rows0, rows1 = left[p], right[p]
        col = [lanes(rows0, 8 * p + j) for j in range(8)]
        s = {(i, j): sublanes(col[j], i) for j in range(8) for i in range(j, 8)}
        later = range(p + 1, count)
        cols = {q: [lanes(left[q], 8 * p + j) for j in range(8)] for q in later}
        for j in range(8):
            r = reciprocal(s[j, j])
            m = {i: s[i, j] * r for i in range(j + 1, 8)}
            for k in range(j + 1, 8):
                for i in range(k, 8):
                    s[i, k] = s[i, k] - m[i] * s[k, j]
            mine = jnp.where(sub > j, col[j] * r, 0.0)
            row0, row1 = sublanes(rows0, j), sublanes(rows1, j)
            for k in range(j + 1, 8):
                col[k] = col[k] - mine * s[k, j]
            rows0 = rows0 - mine * row0
            rows1 = rows1 - mine * row1
            for q in later:
                theirs = cols[q][j] * r
                for k in range(j + 1, 8):
                    cols[q][k] = cols[q][k] - theirs * s[k, j]
                left[q] = left[q] - theirs * row0
                right[q] = right[q] - theirs * row1
        pivots = s[0, 0]
        for i in range(1, 8):
            pivots = jnp.where(sub == i, s[i, i], pivots)
        scale = lax.rsqrt(pivots)
        upper.append(jnp.where(lane >= sub + 8 * p, rows0 * scale, 0.0))
        inverse.append(rows1 * scale)
    return upper, inverse


def panels_of(matrix):
    return [matrix[8 * p : 8 * p + 8, :] for p in range(matrix.shape[0] // 8)]


def exact(a, b, dims=((1,), (0,))):
    return lax.dot_general(
        a, b, (dims, ((), ())), precision=HIGHEST, preferred_element_type=jnp.float32
    )


def orthonormal_steps(g_ref, seed_ref, basis_ref, gram):
    for n, (k, l) in enumerate(PAIRS):
        block = g_ref[n]
        gram[W * k : W * k + W, W * l : W * l + W] = block
        if k != l:
            gram[W * l : W * l + W, W * k : W * k + W] = block.T
    basis_ref[...] = seed_ref[...].T

    def step(_, carry):
        imaged = exact(basis_ref[...], gram[...])
        small = exact(imaged, imaged, ((1,), (1,)))
        _, inverse = factor(panels_of(small))
        basis_ref[...] = exact(jnp.concatenate(inverse, axis=0), imaged)
        return carry

    lax.fori_loop(0, ITERS, step, 0)


def triangle_steps(g_ref, out_ref, rest):
    out_ref[...] = jnp.zeros_like(out_ref)
    for n, (k, l) in enumerate(PAIRS):
        rest[W * k : W * k + W, W * l : W * l + W] = g_ref[n]

    def step(b, carry):
        start = pl.multiple_of(b * W, W)
        own = pl.ds(start, W)
        upper, inverse = factor([rest[pl.ds(start + 8 * p, 8), own] for p in range(W // 8)])
        inverse = jnp.concatenate(inverse, axis=0)

        keep = lax.broadcasted_iota(jnp.int32, (W, NB * W), 1) >= (b + 1) * W
        row = jnp.where(keep, exact(inverse, rest[own, :]), 0.0)
        out_ref[own, :] = row

        def down(c, carry):
            at = pl.ds(pl.multiple_of(c * W, W), W)
            rest[at, :] -= exact(out_ref[own, at].T, out_ref[own, :])
            return carry

        lax.fori_loop(b + 1, NB, down, 0)
        out_ref[own, own] = jnp.concatenate(upper, axis=0)
        return carry

    lax.fori_loop(0, NB - 1, step, 0)
    last = slice(W * (NB - 1), W * NB)
    out_ref[last, last] = rest[last, last]


def copied(*copies):
    for copy in copies:
        copy.start()
    for copy in copies:
        copy.wait()


def either_kernel(core_ref, g_ref, seed_ref, basis_ref, triangle_ref, gram, blocks, seed, basis, triangle, sems):
    copied(
        pltpu.make_async_copy(g_ref, blocks, sems.at[0]),
        pltpu.make_async_copy(seed_ref, seed, sems.at[1]),
    )

    @pl.when(core_ref[0] == 0)
    def _():
        orthonormal_steps(blocks, seed, basis, gram)
        copied(pltpu.make_async_copy(basis, basis_ref, sems.at[2]))

    @pl.when(core_ref[0] != 0)
    def _():
        triangle_steps(blocks, triangle, gram)
        copied(pltpu.make_async_copy(triangle, triangle_ref, sems.at[3]))


def basis_or_triangle(core, gram, seed):
    size = NB * W
    anywhere = pl.BlockSpec(memory_space=pl.ANY)
    return pl.pallas_call(
        either_kernel,
        in_specs=[pl.BlockSpec(memory_space=pltpu.SMEM), anywhere, anywhere],
        out_specs=[anywhere, anywhere],
        out_shape=[
            jax.ShapeDtypeStruct(seed.shape[::-1], jnp.float32),
            jax.ShapeDtypeStruct((size, size), jnp.float32),
        ],
        scratch_shapes=[
            pltpu.VMEM((size, size), jnp.float32),
            pltpu.VMEM(gram.shape, jnp.float32),
            pltpu.VMEM(seed.shape, jnp.float32),
            pltpu.VMEM(seed.shape[::-1], jnp.float32),
            pltpu.VMEM((size, size), jnp.float32),
            pltpu.SemaphoreType.DMA((4,)),
        ],
        compiler_params=pltpu.CompilerParams(vmem_limit_bytes=VMEM_LIMIT),
        cost_estimate=pl.CostEstimate(
            flops=40_000_000_000, bytes_accessed=8 * size * size, transcendentals=0
        ),
        name="basis_or_triangle",
    )(core, gram, seed)


def finish_kernel(core_ref, own_ref, other_ref, out_ref, triangle, sems):
    for flag, source in enumerate((other_ref, own_ref)):

        @pl.when(core_ref[0] == flag)
        def _(source=source):
            copied(pltpu.make_async_copy(source, triangle, sems.at[0]))

    last = slice(W * (NB - 1), W * NB)
    upper, _ = factor(panels_of(triangle[last, last]))
    triangle[last, last] = jnp.concatenate(upper, axis=0)
    copied(pltpu.make_async_copy(triangle, out_ref, sems.at[1]))


def finished(core, own, other):
    anywhere = pl.BlockSpec(memory_space=pl.ANY)
    return pl.pallas_call(
        finish_kernel,
        in_specs=[pl.BlockSpec(memory_space=pltpu.SMEM), anywhere, anywhere],
        out_specs=anywhere,
        out_shape=jax.ShapeDtypeStruct(own.shape, jnp.float32),
        scratch_shapes=[pltpu.VMEM(own.shape, jnp.float32), pltpu.SemaphoreType.DMA((2,))],
        compiler_params=pltpu.CompilerParams(vmem_limit_bytes=VMEM_LIMIT // 6),
        cost_estimate=pl.CostEstimate(
            flops=6_000_000_000, bytes_accessed=8 * own.size, transcendentals=0
        ),
        name="finished",
    )(core, own, other)


def core_kernel(counts, snaps, me_ref, own_ref, other_ref, *refs):
    n = 2 * len(counts)
    sources, refs = refs[:n], refs[n:]
    mode_ref, *out_refs = refs[: 1 + NB]
    refs = refs[1 + NB :]
    halves, (basis, mode, parts, in_sems, out_sems) = refs[:n], refs[n:]
    me, part = me_ref[0], basis.shape[0] // NB
    arrivals = [
        pltpu.make_async_copy(source, half, in_sems.at[i])
        for i, (source, half) in enumerate(zip(sources, halves))
    ]

    for copy in arrivals:
        copy.start()

    @pl.when(me_ref[1] == 0)
    def _():
        copied(pltpu.make_async_copy(own_ref, basis, in_sems.at[n]))

    @pl.when(me_ref[1] != 0)
    def _():
        copied(pltpu.make_async_copy(other_ref, basis, in_sems.at[n]))

    mode[...] = basis[...].T
    leaving = [pltpu.make_async_copy(mode, mode_ref, out_sems.at[NB])]
    leaving[0].start()
    turned = [basis[pl.ds(pl.multiple_of((me ^ b) * part, part), part), :] for b in range(NB)]
    high, low = split(jnp.concatenate(turned, axis=0).T)
    weights = jnp.concatenate([high, low], axis=1)
    cell = 0
    for c, count in enumerate(counts):
        high_ref, low_ref = halves[2 * c : 2 * c + 2]
        arrivals[2 * c].wait()
        arrivals[2 * c + 1].wait()
        for i in range(count):
            rows = slice(snaps * i, snaps * i + snaps)
            both = contract(high_ref[rows, :], weights, ((1,), (0,)))
            more = contract(low_ref[rows, :], high, ((1,), (0,)))
            core = (both[:, :W] + (both[:, W:] + more)).T
            for b in range(NB):
                parts[b, cell] = core[part * b : part * b + part, :]
            cell += 1
    for b in range(NB):
        leaving.append(pltpu.make_async_copy(parts.at[b], out_refs[b], out_sems.at[b]))
        leaving[-1].start()
    for copy in leaving:
        copy.wait()


def core_parts(place, own_basis, other_basis, halves, counts, snaps):
    rank, size = own_basis.shape
    cells = sum(counts)
    operands = [half for pair in halves for half in pair]
    anywhere = pl.BlockSpec(memory_space=pl.ANY)
    return pl.pallas_call(
        lambda *refs: core_kernel(counts, snaps, *refs),
        in_specs=[pl.BlockSpec(memory_space=pltpu.SMEM)] + [anywhere] * (2 + len(operands)),
        out_specs=[anywhere] * (1 + NB),
        out_shape=[jax.ShapeDtypeStruct((size, rank), jnp.float32)]
        + [jax.ShapeDtypeStruct((cells, rank // NB, snaps), jnp.float32)] * NB,
        scratch_shapes=[pltpu.VMEM(half.shape, half.dtype) for half in operands]
        + [
            pltpu.VMEM((rank, size), jnp.float32),
            pltpu.VMEM((size, rank), jnp.float32),
            pltpu.VMEM((NB, cells, rank // NB, snaps), jnp.float32),
            pltpu.SemaphoreType.DMA((len(operands) + 1,)),
            pltpu.SemaphoreType.DMA((NB + 1,)),
        ],
        compiler_params=pltpu.CompilerParams(vmem_limit_bytes=VMEM_LIMIT),
        cost_estimate=pl.CostEstimate(
            flops=6 * cells * snaps * size * rank,
            bytes_accessed=5 * cells * snaps * size,
            transcendentals=0,
        ),
        name="core_parts",
    )(place, own_basis, other_basis, *operands)


def placed_kernel(me_ref, *refs):
    parts, (out_ref, held, sems) = refs[:NB], refs[NB:]
    arrivals = [
        pltpu.make_async_copy(part, held.at[b], sems.at[b]) for b, part in enumerate(parts)
    ]
    leaving = [
        pltpu.make_async_copy(held.at[b], out_ref.at[me_ref[0] ^ b], sems.at[NB + b])
        for b in range(NB)
    ]
    for copy in arrivals:
        copy.start()
    for arrival, copy in zip(arrivals, leaving):
        arrival.wait()
        copy.start()
    for copy in leaving:
        copy.wait()


def placed(me, parts):
    anywhere = pl.BlockSpec(memory_space=pl.ANY)
    return pl.pallas_call(
        placed_kernel,
        in_specs=[pl.BlockSpec(memory_space=pltpu.SMEM)] + [anywhere] * NB,
        out_specs=anywhere,
        out_shape=jax.ShapeDtypeStruct((NB, *parts[0].shape), jnp.float32),
        scratch_shapes=[
            pltpu.VMEM((NB, *parts[0].shape), jnp.float32),
            pltpu.SemaphoreType.DMA((2 * NB,)),
        ],
        compiler_params=pltpu.CompilerParams(vmem_limit_bytes=VMEM_LIMIT // 6),
        name="placed",
    )(me, *parts)


def exchanged(block, axis, bits):
    count = lax.axis_size(axis)
    return lax.ppermute(block, axis, [(i, i ^ bits) for i in range(count)])


def summed_over_devices(part):
    half = part.shape[0] // 2
    core = lax.axis_index("core")
    keep = lax.dynamic_slice_in_dim(part, core * half, half, 0)
    send = lax.dynamic_slice_in_dim(part, (1 - core) * half, half, 0)
    own = keep + exchanged(send, "core", 1)
    shares = lax.all_to_all(
        own.reshape(NB, half // NB, W), "x", split_axis=0, concat_axis=0, tiled=True
    )
    own = (shares[0] + shares[1]) + (shares[2] + shares[3])
    two, one, three = (exchanged(own, "y", bits) for bits in (2, 1, 3))
    own = (own + one) + (two + three)
    own = own + exchanged(own, "z", 1)
    four, two, six = (exchanged(own, "z", bits) for bits in (4, 2, 6))
    own = (own + two) + (four + six)
    copies = jnp.broadcast_to(own[None], (NB, *own.shape))
    whole = lax.all_to_all(copies, "x", split_axis=0, concat_axis=0, tiled=True)
    whole = whole.reshape(half, W)
    return lax.all_gather(whole, "core", axis=0, tiled=True)


def local(soil_heat_field, seed_subspace):
    cells, snaps, width = soil_heat_field.shape
    devices = lax.axis_size(("x", "y", "z", "core"))
    me, core = lax.axis_index("x"), lax.axis_index("core")
    place = jnp.stack([me, core]).astype(jnp.int32)
    field = soil_heat_field.reshape(NB, cells // NB, snaps, width)
    scale = 1.0 / (cells // NB * snaps * devices)
    counts = COUNTS

    gram, halves, start = None, [], 0
    arrived = []
    for c, count in enumerate(counts):
        later, got = field, {}
        if c >= 2:
            later, *arrived[c - 2] = lax.optimization_barrier((field, *arrived[c - 2]))
        for bits in (2, 1, 3):
            send = lax.dynamic_slice(
                later, (me ^ bits, start, 0, 0), (1, count, snaps, width)
            )[0]
            got[bits] = exchanged(send, "x", bits)
        arrived.append([got[bits] for bits in (1, 2, 3)])
        start += count
    start = 0
    for count, others in zip(counts, arrived):
        gram, high, low = gram_chunk(place, field, start, count, others, gram, scale)
        halves.append((high, low))
        start += count

    gram = summed_over_devices(gram.reshape(-1, W)).reshape(gram.shape)
    basis, triangle = basis_or_triangle(place[1:], gram, seed_subspace)
    other_basis = exchanged(basis, "core", 1)
    triangle, other_basis = lax.optimization_barrier((triangle, other_basis))
    other_triangle = exchanged(triangle, "core", 1)
    mode_factor, *parts = core_parts(place, basis, other_basis, halves, counts, snaps)
    sent = {bits: exchanged(parts[bits], "x", bits) for bits in (2, 1, 3)}
    triangle = finished(place[1:], triangle, other_triangle)
    own_part, triangle = lax.optimization_barrier((parts[0], triangle))
    core_tensor = placed(place, [own_part] + [sent[bits] for bits in (1, 2, 3)])
    core_tensor = core_tensor.reshape(cells, -1, snaps).transpose(0, 2, 1)
    return (core_tensor, mode_factor, triangle)


def solution(mesh):
    fine = Mesh(mesh.devices.reshape(4, -1, 8, 2), ("x", "y", "z", "core"))
    cell = ("y", "z", "core")
    return jax.shard_map(
        local,
        mesh=fine,
        in_specs=(P(cell, None, "x"), P()),
        out_specs=(P(cell, None, "x"), P(), P()),
        check_vma=False,
    )
```

```python
import jax
import jax.numpy as jnp
from jax import lax
from jax.experimental import pallas as pl
from jax.experimental.pallas import tpu as pltpu
from jax.sharding import Mesh, PartitionSpec as P

ITERS = 3
HIGHEST = lax.Precision.HIGHEST
NB = 4
W = 128
PAIRS = [(k, l) for k in range(NB) for l in range(k, NB)]
COUNTS = (2, 6)
STEP = 2
SMALL = 14 * 1024 * 1024
VMEM_LIMIT = 60 * 1024 * 1024


def split(x):
    high = x.astype(jnp.bfloat16)
    return high, (x - high.astype(jnp.float32)).astype(jnp.bfloat16)


def contract(a, b, dims):
    return lax.dot_general(a, b, (dims, ((), ())), preferred_element_type=jnp.float32)


def gram_kernel(scale, counts, me_ref, field, *refs):
    count = (NB - 1) * len(counts)
    others, refs = refs[:count], refs[count:]
    out_ref, high_ref, low_ref, rows, high, low, hh, hl, total, in_sems, out_sems = refs
    _, snaps, size = rows.shape
    me = me_ref[0]
    groups, start = [], 0
    for c, cells in enumerate(counts):
        groups += [(c, at, start + at) for at in range(0, cells, STEP)]
        start += cells
    arrivals = []
    for g, (c, at, cell) in enumerate(groups):
        pieces = [field.at[me, pl.ds(cell, STEP)]]
        pieces += [ref.at[pl.ds(at, STEP)] for ref in others[(NB - 1) * c : (NB - 1) * (c + 1)]]
        arrivals.append([])
        for b, piece in enumerate(pieces):
            place = pl.multiple_of((me ^ b) * W, W)
            target = rows.at[pl.ds(cell, STEP), :, pl.ds(place, W)]
            arrivals[g].append(pltpu.make_async_copy(piece, target, in_sems.at[g, b]))
            arrivals[g][b].start()
    leaving = []
    for g, (_, _, cell) in enumerate(groups):
        for copy in arrivals[g]:
            copy.wait()
        at = slice(cell * snaps, (cell + STEP) * snaps)
        part, rest = split(rows[cell : cell + STEP].reshape(STEP * snaps, size))
        high[at, :], low[at, :] = part, rest
        for n, (source, target) in enumerate(((high, high_ref), (low, low_ref))):
            leaving.append(pltpu.make_async_copy(source.at[at], target.at[at], out_sems.at[g, n]))
            leaving[-1].start()
        left = part.T
        for total_ref, right in ((hh, part), (hl, rest)):
            product = contract(left, right, ((1,), (0,)))
            total_ref[...] = product if g == 0 else total_ref[...] + product
    for n, (k, l) in enumerate(PAIRS):
        ks, ls = slice(W * k, W * k + W), slice(W * l, W * l + W)
        total[n] = (hh[ks, ls] + (hl[ks, ls] + hl[ls, ks].T)) * scale
    leaving.append(pltpu.make_async_copy(total, out_ref, out_sems.at[len(groups), 0]))
    leaving[-1].start()
    for copy in leaving:
        copy.wait()


def gram_blocks(me, field, counts, arrived, scale):
    _, cells, snaps, _ = field.shape
    rows, size = cells * snaps, NB * W
    gram = (len(PAIRS), W, W)
    halves = jax.ShapeDtypeStruct((rows, size), jnp.bfloat16)
    anywhere = pl.BlockSpec(memory_space=pl.ANY)
    operands = [field] + [piece for pieces in arrived for piece in pieces]
    return pl.pallas_call(
        lambda *refs: gram_kernel(scale, counts, *refs),
        in_specs=[pl.BlockSpec(memory_space=pltpu.SMEM)] + [anywhere] * len(operands),
        out_specs=[anywhere] * 3,
        out_shape=[jax.ShapeDtypeStruct(gram, jnp.float32), halves, halves],
        scratch_shapes=[
            pltpu.VMEM((cells, snaps, size), jnp.float32),
            pltpu.VMEM(halves.shape, jnp.bfloat16),
            pltpu.VMEM(halves.shape, jnp.bfloat16),
            pltpu.VMEM((size, size), jnp.float32),
            pltpu.VMEM((size, size), jnp.float32),
            pltpu.VMEM(gram, jnp.float32),
            pltpu.SemaphoreType.DMA((cells // STEP, NB)),
            pltpu.SemaphoreType.DMA((cells // STEP + 1, 2)),
        ],
        compiler_params=pltpu.CompilerParams(vmem_limit_bytes=VMEM_LIMIT),
        cost_estimate=pl.CostEstimate(
            flops=4 * rows * size**2, bytes_accessed=8 * rows * size, transcendentals=0
        ),
        name="gram_blocks",
    )(me, *operands)


def reciprocal(d):
    r = pltpu.reciprocal(d, approx=True)
    return r * (2.0 - d * r)


def lanes(x, l):
    return jnp.broadcast_to(x[:, l : l + 1], (8, W))


def sublanes(x, i):
    return jnp.broadcast_to(x[i : i + 1, :], (8, W))


def factor(panels):
    count = len(panels)
    left = list(panels)
    sub = lax.broadcasted_iota(jnp.int32, (8, W), 0)
    lane = lax.broadcasted_iota(jnp.int32, (8, W), 1)
    right = [jnp.where(lane == sub + 8 * p, 1.0, 0.0).astype(jnp.float32) for p in range(count)]
    upper, inverse = [], []
    for p in range(count):
        rows0, rows1 = left[p], right[p]
        col = [lanes(rows0, 8 * p + j) for j in range(8)]
        s = {(i, j): sublanes(col[j], i) for j in range(8) for i in range(j, 8)}
        later = range(p + 1, count)
        cols = {q: [lanes(left[q], 8 * p + j) for j in range(8)] for q in later}
        for j in range(8):
            r = reciprocal(s[j, j])
            m = {i: s[i, j] * r for i in range(j + 1, 8)}
            for k in range(j + 1, 8):
                for i in range(k, 8):
                    s[i, k] = s[i, k] - m[i] * s[k, j]
            mine = jnp.where(sub > j, col[j] * r, 0.0)
            row0, row1 = sublanes(rows0, j), sublanes(rows1, j)
            for k in range(j + 1, 8):
                col[k] = col[k] - mine * s[k, j]
            rows0 = rows0 - mine * row0
            rows1 = rows1 - mine * row1
            for q in later:
                theirs = cols[q][j] * r
                for k in range(j + 1, 8):
                    cols[q][k] = cols[q][k] - theirs * s[k, j]
                left[q] = left[q] - theirs * row0
                right[q] = right[q] - theirs * row1
        pivots = s[0, 0]
        for i in range(1, 8):
            pivots = jnp.where(sub == i, s[i, i], pivots)
        scale = lax.rsqrt(pivots)
        upper.append(jnp.where(lane >= sub + 8 * p, rows0 * scale, 0.0))
        inverse.append(rows1 * scale)
    return upper, inverse


def panels_of(matrix):
    return [matrix[8 * p : 8 * p + 8, :] for p in range(matrix.shape[0] // 8)]


def exact(a, b, dims=((1,), (0,))):
    return lax.dot_general(
        a, b, (dims, ((), ())), precision=HIGHEST, preferred_element_type=jnp.float32
    )


def orthonormal_steps(g_ref, seed_ref, basis_ref, gram):
    for n, (k, l) in enumerate(PAIRS):
        block = g_ref[n]
        gram[W * k : W * k + W, W * l : W * l + W] = block
        if k != l:
            gram[W * l : W * l + W, W * k : W * k + W] = block.T
    basis_ref[...] = seed_ref[...]

    def step(_, carry):
        imaged = exact(basis_ref[...], gram[...])
        small = exact(imaged, imaged, ((1,), (1,)))
        _, inverse = factor(panels_of(small))
        basis_ref[...] = exact(jnp.concatenate(inverse, axis=0), imaged)
        return carry

    lax.fori_loop(0, ITERS, step, 0)


def triangle_steps(g_ref, out_ref, rest):
    out_ref[...] = jnp.zeros_like(out_ref)
    for n, (k, l) in enumerate(PAIRS):
        rest[W * k : W * k + W, W * l : W * l + W] = g_ref[n]

    def step(b, carry):
        start = pl.multiple_of(b * W, W)
        own = pl.ds(start, W)
        upper, inverse = factor([rest[pl.ds(start + 8 * p, 8), own] for p in range(W // 8)])
        inverse = jnp.concatenate(inverse, axis=0)

        keep = lax.broadcasted_iota(jnp.int32, (W, NB * W), 1) >= (b + 1) * W
        row = jnp.where(keep, exact(inverse, rest[own, :]), 0.0)
        out_ref[own, :] = row

        def down(c, carry):
            at = pl.ds(pl.multiple_of(c * W, W), W)
            rest[at, :] -= exact(out_ref[own, at].T, out_ref[own, :])
            return carry

        lax.fori_loop(b + 1, NB, down, 0)
        out_ref[own, own] = jnp.concatenate(upper, axis=0)
        return carry

    lax.fori_loop(0, NB - 1, step, 0)
    last = slice(W * (NB - 1), W * NB)
    out_ref[last, last] = rest[last, last]


def copied(*copies):
    for copy in copies:
        copy.start()
    for copy in copies:
        copy.wait()


def either_kernel(core_ref, g_ref, seed_ref, basis_ref, triangle_ref, gram):
    @pl.when(core_ref[0] == 0)
    def _():
        orthonormal_steps(g_ref, seed_ref, basis_ref, gram)

    @pl.when(core_ref[0] != 0)
    def _():
        triangle_steps(g_ref, triangle_ref, gram)


def basis_or_triangle(core, gram, seed_rows):
    size = NB * W
    vmem = pl.BlockSpec(memory_space=pltpu.VMEM)
    return pl.pallas_call(
        either_kernel,
        in_specs=[pl.BlockSpec(memory_space=pltpu.SMEM), vmem, vmem],
        out_specs=[vmem, vmem],
        out_shape=[
            jax.ShapeDtypeStruct(seed_rows.shape, jnp.float32),
            jax.ShapeDtypeStruct((size, size), jnp.float32),
        ],
        scratch_shapes=[pltpu.VMEM((size, size), jnp.float32)],
        compiler_params=pltpu.CompilerParams(vmem_limit_bytes=SMALL),
        cost_estimate=pl.CostEstimate(
            flops=40_000_000_000, bytes_accessed=8 * size * size, transcendentals=0
        ),
        name="basis_or_triangle",
    )(core, gram, seed_rows)


def finish_kernel(core_ref, own_ref, other_ref, out_ref, triangle, sems):
    for flag, source in enumerate((other_ref, own_ref)):

        @pl.when(core_ref[0] == flag)
        def _(source=source):
            copied(pltpu.make_async_copy(source, triangle, sems.at[0]))

    last = slice(W * (NB - 1), W * NB)
    upper, _ = factor(panels_of(triangle[last, last]))
    triangle[last, last] = jnp.concatenate(upper, axis=0)
    copied(pltpu.make_async_copy(triangle, out_ref, sems.at[1]))


def finished(core, own, other):
    anywhere = pl.BlockSpec(memory_space=pl.ANY)
    return pl.pallas_call(
        finish_kernel,
        in_specs=[pl.BlockSpec(memory_space=pltpu.SMEM), anywhere, anywhere],
        out_specs=anywhere,
        out_shape=jax.ShapeDtypeStruct(own.shape, jnp.float32),
        scratch_shapes=[pltpu.VMEM(own.shape, jnp.float32), pltpu.SemaphoreType.DMA((2,))],
        compiler_params=pltpu.CompilerParams(vmem_limit_bytes=VMEM_LIMIT // 6),
        cost_estimate=pl.CostEstimate(
            flops=6_000_000_000, bytes_accessed=8 * own.size, transcendentals=0
        ),
        name="finished",
    )(core, own, other)


def core_kernel(counts, snaps, me_ref, own_ref, other_ref, *refs):
    halves, (mode_ref, *outs), basis = refs[: 2 * len(counts)], refs[2 * len(counts) : -1], refs[-1]
    me, part = me_ref[0], own_ref.shape[0] // NB
    basis[...] = jnp.where(me_ref[1] == 0, own_ref[...], other_ref[...])
    mode_ref[...] = basis[...].T
    turned = [basis[pl.ds(pl.multiple_of((me ^ b) * part, part), part), :] for b in range(NB)]
    high, low = split(jnp.concatenate(turned, axis=0).T)
    weights = jnp.concatenate([high, low], axis=1)
    cell = 0
    for c, count in enumerate(counts):
        high_ref, low_ref = halves[2 * c : 2 * c + 2]
        for i in range(count):
            rows = slice(snaps * i, snaps * i + snaps)
            both = contract(high_ref[rows, :], weights, ((1,), (0,)))
            more = contract(low_ref[rows, :], high, ((1,), (0,)))
            core = (both[:, :W] + (both[:, W:] + more)).T
            for b in range(NB):
                outs[b][cell] = core[part * b : part * b + part, :]
            cell += 1


def core_parts(place, own_basis, other_basis, halves, counts, snaps):
    rank, size = own_basis.shape
    cells = sum(counts)
    operands = [half for pair in halves for half in pair]
    vmem = pl.BlockSpec(memory_space=pltpu.VMEM)
    return pl.pallas_call(
        lambda *refs: core_kernel(counts, snaps, *refs),
        in_specs=[pl.BlockSpec(memory_space=pltpu.SMEM)] + [vmem] * (2 + len(operands)),
        out_specs=[vmem] * (1 + NB),
        out_shape=[jax.ShapeDtypeStruct((size, rank), jnp.float32)]
        + [jax.ShapeDtypeStruct((cells, rank // NB, snaps), jnp.float32)] * NB,
        scratch_shapes=[pltpu.VMEM((rank, size), jnp.float32)],
        compiler_params=pltpu.CompilerParams(vmem_limit_bytes=SMALL),
        cost_estimate=pl.CostEstimate(
            flops=6 * cells * snaps * size * rank,
            bytes_accessed=5 * cells * snaps * size,
            transcendentals=0,
        ),
        name="core_parts",
    )(place, own_basis, other_basis, *operands)


def placed_kernel(me_ref, *refs):
    parts, (out_ref, held, sems) = refs[:NB], refs[NB:]
    arrivals = [
        pltpu.make_async_copy(part, held.at[b], sems.at[b]) for b, part in enumerate(parts)
    ]
    leaving = [
        pltpu.make_async_copy(held.at[b], out_ref.at[me_ref[0] ^ b], sems.at[NB + b])
        for b in range(NB)
    ]
    for copy in arrivals:
        copy.start()
    for arrival, copy in zip(arrivals, leaving):
        arrival.wait()
        copy.start()
    for copy in leaving:
        copy.wait()


def placed(me, parts):
    anywhere = pl.BlockSpec(memory_space=pl.ANY)
    return pl.pallas_call(
        placed_kernel,
        in_specs=[pl.BlockSpec(memory_space=pltpu.SMEM)] + [anywhere] * NB,
        out_specs=anywhere,
        out_shape=jax.ShapeDtypeStruct((NB, *parts[0].shape), jnp.float32),
        scratch_shapes=[
            pltpu.VMEM((NB, *parts[0].shape), jnp.float32),
            pltpu.SemaphoreType.DMA((2 * NB,)),
        ],
        compiler_params=pltpu.CompilerParams(vmem_limit_bytes=VMEM_LIMIT // 6),
        name="placed",
    )(me, *parts)


def exchanged(block, axis, bits):
    count = lax.axis_size(axis)
    return lax.ppermute(block, axis, [(i, i ^ bits) for i in range(count)])


def summed_over_devices(part):
    half = part.shape[0] // 2
    core = lax.axis_index("core")
    keep = lax.dynamic_slice_in_dim(part, core * half, half, 0)
    send = lax.dynamic_slice_in_dim(part, (1 - core) * half, half, 0)
    own = keep + exchanged(send, "core", 1)
    shares = lax.all_to_all(
        own.reshape(NB, half // NB, W), "x", split_axis=0, concat_axis=0, tiled=True
    )
    own = (shares[0] + shares[1]) + (shares[2] + shares[3])
    two, one, three = (exchanged(own, "y", bits) for bits in (2, 1, 3))
    own = (own + one) + (two + three)
    own = own + exchanged(own, "z", 1)
    four, two, six = (exchanged(own, "z", bits) for bits in (4, 2, 6))
    own = (own + two) + (four + six)
    copies = jnp.broadcast_to(own[None], (NB, *own.shape))
    whole = lax.all_to_all(copies, "x", split_axis=0, concat_axis=0, tiled=True)
    whole = whole.reshape(half, W)
    return lax.all_gather(whole, "core", axis=0, tiled=True)


def local(soil_heat_field, seed_subspace):
    cells, snaps, width = soil_heat_field.shape
    devices = lax.axis_size(("x", "y", "z", "core"))
    me, core = lax.axis_index("x"), lax.axis_index("core")
    place = jnp.stack([me, core]).astype(jnp.int32)
    field = soil_heat_field.reshape(NB, cells // NB, snaps, width)
    scale = 1.0 / (cells // NB * snaps * devices)
    counts = COUNTS

    arrived, start, later = [], 0, field
    for count in counts:
        got, sends = {}, []
        for bits in (2, 1, 3):
            send = lax.dynamic_slice(later, (me ^ bits, start, 0, 0), (1, count, snaps, width))[0]
            got[bits] = exchanged(send, "x", bits)
            sends.append(send)
        later, *_ = lax.optimization_barrier((later, *sends))
        arrived.append([got[bits] for bits in (1, 2, 3)])
        start += count
    gram, high, low = gram_blocks(place, field, counts, arrived, scale)

    gram = summed_over_devices(gram.reshape(-1, W)).reshape(gram.shape)
    basis, triangle = basis_or_triangle(place[1:], gram, seed_subspace.T)
    other_basis = exchanged(basis, "core", 1)
    triangle, other_basis = lax.optimization_barrier((triangle, other_basis))
    other_triangle = exchanged(triangle, "core", 1)
    mode_factor, *parts = core_parts(
        place, basis, other_basis, [(high, low)], [cells // NB], snaps
    )
    sent = {bits: exchanged(parts[bits], "x", bits) for bits in (2, 1, 3)}
    triangle = finished(place[1:], triangle, other_triangle)
    own_part, triangle = lax.optimization_barrier((parts[0], triangle))
    core_tensor = placed(place, [own_part] + [sent[bits] for bits in (1, 2, 3)])
    core_tensor = core_tensor.reshape(cells, -1, snaps).transpose(0, 2, 1)
    return (core_tensor, mode_factor, triangle)


def solution(mesh):
    fine = Mesh(mesh.devices.reshape(4, -1, 8, 2), ("x", "y", "z", "core"))
    cell = ("y", "z", "core")
    return jax.shard_map(
        local,
        mesh=fine,
        in_specs=(P(cell, None, "x"), P()),
        out_specs=(P(cell, None, "x"), P(), P()),
        check_vma=False,
    )
```

```python
import jax
import jax.numpy as jnp
from jax import lax
from jax.experimental import pallas as pl
from jax.experimental.pallas import tpu as pltpu
from jax.sharding import Mesh, PartitionSpec as P

ITERS = 3
HIGHEST = lax.Precision.HIGHEST
NB = 4
W = 128
PAIRS = [(k, l) for k in range(NB) for l in range(k, NB)]
COUNTS = (8,)
STEP = 2
SMALL = 14 * 1024 * 1024
VMEM_LIMIT = 60 * 1024 * 1024


def split(x):
    high = x.astype(jnp.bfloat16)
    return high, (x - high.astype(jnp.float32)).astype(jnp.bfloat16)


def contract(a, b, dims):
    return lax.dot_general(a, b, (dims, ((), ())), preferred_element_type=jnp.float32)


def gram_kernel(scale, counts, me_ref, field, *refs):
    count = (NB - 1) * len(counts)
    others, refs = refs[:count], refs[count:]
    out_ref, high_ref, low_ref, rows, high, low, hh, hl, total, in_sems, out_sems = refs
    _, snaps, size = rows.shape
    me = me_ref[0]
    groups, start = [], 0
    for c, cells in enumerate(counts):
        groups += [(c, at, start + at) for at in range(0, cells, STEP)]
        start += cells
    arrivals = []
    for g, (c, at, cell) in enumerate(groups):
        pieces = [field.at[me, pl.ds(cell, STEP)]]
        pieces += [ref.at[pl.ds(at, STEP)] for ref in others[(NB - 1) * c : (NB - 1) * (c + 1)]]
        arrivals.append([])
        for b, piece in enumerate(pieces):
            place = pl.multiple_of((me ^ b) * W, W)
            target = rows.at[pl.ds(cell, STEP), :, pl.ds(place, W)]
            arrivals[g].append(pltpu.make_async_copy(piece, target, in_sems.at[g, b]))
            arrivals[g][b].start()
    leaving = []
    for g, (_, _, cell) in enumerate(groups):
        for copy in arrivals[g]:
            copy.wait()
        at = slice(cell * snaps, (cell + STEP) * snaps)
        part, rest = split(rows[cell : cell + STEP].reshape(STEP * snaps, size))
        high[at, :], low[at, :] = part, rest
        for n, (source, target) in enumerate(((high, high_ref), (low, low_ref))):
            leaving.append(pltpu.make_async_copy(source.at[at], target.at[at], out_sems.at[g, n]))
            leaving[-1].start()
        left = part.T
        for total_ref, right in ((hh, part), (hl, rest)):
            product = contract(left, right, ((1,), (0,)))
            total_ref[...] = product if g == 0 else total_ref[...] + product
    for n, (k, l) in enumerate(PAIRS):
        ks, ls = slice(W * k, W * k + W), slice(W * l, W * l + W)
        total[n] = (hh[ks, ls] + (hl[ks, ls] + hl[ls, ks].T)) * scale
    leaving.append(pltpu.make_async_copy(total, out_ref, out_sems.at[len(groups), 0]))
    leaving[-1].start()
    for copy in leaving:
        copy.wait()


def gram_blocks(me, field, counts, arrived, scale):
    _, cells, snaps, _ = field.shape
    rows, size = cells * snaps, NB * W
    gram = (len(PAIRS), W, W)
    halves = jax.ShapeDtypeStruct((rows, size), jnp.bfloat16)
    anywhere = pl.BlockSpec(memory_space=pl.ANY)
    operands = [field] + [piece for pieces in arrived for piece in pieces]
    return pl.pallas_call(
        lambda *refs: gram_kernel(scale, counts, *refs),
        in_specs=[pl.BlockSpec(memory_space=pltpu.SMEM)] + [anywhere] * len(operands),
        out_specs=[anywhere] * 3,
        out_shape=[jax.ShapeDtypeStruct(gram, jnp.float32), halves, halves],
        scratch_shapes=[
            pltpu.VMEM((cells, snaps, size), jnp.float32),
            pltpu.VMEM(halves.shape, jnp.bfloat16),
            pltpu.VMEM(halves.shape, jnp.bfloat16),
            pltpu.VMEM((size, size), jnp.float32),
            pltpu.VMEM((size, size), jnp.float32),
            pltpu.VMEM(gram, jnp.float32),
            pltpu.SemaphoreType.DMA((cells // STEP, NB)),
            pltpu.SemaphoreType.DMA((cells // STEP + 1, 2)),
        ],
        compiler_params=pltpu.CompilerParams(vmem_limit_bytes=VMEM_LIMIT),
        cost_estimate=pl.CostEstimate(
            flops=4 * rows * size**2, bytes_accessed=8 * rows * size, transcendentals=0
        ),
        name="gram_blocks",
    )(me, *operands)


def reciprocal(d):
    r = pltpu.reciprocal(d, approx=True)
    return r * (2.0 - d * r)


def lanes(x, l):
    return jnp.broadcast_to(x[:, l : l + 1], (8, W))


def sublanes(x, i):
    return jnp.broadcast_to(x[i : i + 1, :], (8, W))


def factor(panels):
    count = len(panels)
    left = list(panels)
    sub = lax.broadcasted_iota(jnp.int32, (8, W), 0)
    lane = lax.broadcasted_iota(jnp.int32, (8, W), 1)
    right = [jnp.where(lane == sub + 8 * p, 1.0, 0.0).astype(jnp.float32) for p in range(count)]
    upper, inverse = [], []
    for p in range(count):
        rows0, rows1 = left[p], right[p]
        col = [lanes(rows0, 8 * p + j) for j in range(8)]
        s = {(i, j): sublanes(col[j], i) for j in range(8) for i in range(j, 8)}
        later = range(p + 1, count)
        cols = {q: [lanes(left[q], 8 * p + j) for j in range(8)] for q in later}
        for j in range(8):
            r = reciprocal(s[j, j])
            m = {i: s[i, j] * r for i in range(j + 1, 8)}
            for k in range(j + 1, 8):
                for i in range(k, 8):
                    s[i, k] = s[i, k] - m[i] * s[k, j]
            mine = jnp.where(sub > j, col[j] * r, 0.0)
            row0, row1 = sublanes(rows0, j), sublanes(rows1, j)
            for k in range(j + 1, 8):
                col[k] = col[k] - mine * s[k, j]
            rows0 = rows0 - mine * row0
            rows1 = rows1 - mine * row1
            for q in later:
                theirs = cols[q][j] * r
                for k in range(j + 1, 8):
                    cols[q][k] = cols[q][k] - theirs * s[k, j]
                left[q] = left[q] - theirs * row0
                right[q] = right[q] - theirs * row1
        pivots = s[0, 0]
        for i in range(1, 8):
            pivots = jnp.where(sub == i, s[i, i], pivots)
        scale = lax.rsqrt(pivots)
        upper.append(jnp.where(lane >= sub + 8 * p, rows0 * scale, 0.0))
        inverse.append(rows1 * scale)
    return upper, inverse


def panels_of(matrix):
    return [matrix[8 * p : 8 * p + 8, :] for p in range(matrix.shape[0] // 8)]


def exact(a, b, dims=((1,), (0,))):
    return lax.dot_general(
        a, b, (dims, ((), ())), precision=HIGHEST, preferred_element_type=jnp.float32
    )


def orthonormal_steps(g_ref, seed_ref, basis_ref, gram):
    for n, (k, l) in enumerate(PAIRS):
        block = g_ref[n]
        gram[W * k : W * k + W, W * l : W * l + W] = block
        if k != l:
            gram[W * l : W * l + W, W * k : W * k + W] = block.T
    basis_ref[...] = seed_ref[...]

    def step(_, carry):
        imaged = exact(basis_ref[...], gram[...])
        small = exact(imaged, imaged, ((1,), (1,)))
        _, inverse = factor(panels_of(small))
        basis_ref[...] = exact(jnp.concatenate(inverse, axis=0), imaged)
        return carry

    lax.fori_loop(0, ITERS, step, 0)


def triangle_steps(g_ref, out_ref, rest):
    out_ref[...] = jnp.zeros_like(out_ref)
    for n, (k, l) in enumerate(PAIRS):
        rest[W * k : W * k + W, W * l : W * l + W] = g_ref[n]

    def step(b, carry):
        start = pl.multiple_of(b * W, W)
        own = pl.ds(start, W)
        upper, inverse = factor([rest[pl.ds(start + 8 * p, 8), own] for p in range(W // 8)])
        inverse = jnp.concatenate(inverse, axis=0)

        keep = lax.broadcasted_iota(jnp.int32, (W, NB * W), 1) >= (b + 1) * W
        row = jnp.where(keep, exact(inverse, rest[own, :]), 0.0)
        out_ref[own, :] = row

        def down(c, carry):
            at = pl.ds(pl.multiple_of(c * W, W), W)
            rest[at, :] -= exact(out_ref[own, at].T, out_ref[own, :])
            return carry

        lax.fori_loop(b + 1, NB, down, 0)
        out_ref[own, own] = jnp.concatenate(upper, axis=0)
        return carry

    lax.fori_loop(0, NB - 1, step, 0)
    last = slice(W * (NB - 1), W * NB)
    out_ref[last, last] = rest[last, last]


def copied(*copies):
    for copy in copies:
        copy.start()
    for copy in copies:
        copy.wait()


def either_kernel(core_ref, g_ref, seed_ref, basis_ref, triangle_ref, gram):
    @pl.when(core_ref[0] == 0)
    def _():
        orthonormal_steps(g_ref, seed_ref, basis_ref, gram)

    @pl.when(core_ref[0] != 0)
    def _():
        triangle_steps(g_ref, triangle_ref, gram)


def basis_or_triangle(core, gram, seed_rows):
    size = NB * W
    vmem = pl.BlockSpec(memory_space=pltpu.VMEM)
    return pl.pallas_call(
        either_kernel,
        in_specs=[pl.BlockSpec(memory_space=pltpu.SMEM), vmem, vmem],
        out_specs=[vmem, vmem],
        out_shape=[
            jax.ShapeDtypeStruct(seed_rows.shape, jnp.float32),
            jax.ShapeDtypeStruct((size, size), jnp.float32),
        ],
        scratch_shapes=[pltpu.VMEM((size, size), jnp.float32)],
        compiler_params=pltpu.CompilerParams(vmem_limit_bytes=SMALL),
        cost_estimate=pl.CostEstimate(
            flops=40_000_000_000, bytes_accessed=8 * size * size, transcendentals=0
        ),
        name="basis_or_triangle",
    )(core, gram, seed_rows)


def finish_kernel(core_ref, own_ref, other_ref, out_ref, triangle, sems):
    for flag, source in enumerate((other_ref, own_ref)):

        @pl.when(core_ref[0] == flag)
        def _(source=source):
            copied(pltpu.make_async_copy(source, triangle, sems.at[0]))

    last = slice(W * (NB - 1), W * NB)
    upper, _ = factor(panels_of(triangle[last, last]))
    triangle[last, last] = jnp.concatenate(upper, axis=0)
    copied(pltpu.make_async_copy(triangle, out_ref, sems.at[1]))


def finished(core, own, other):
    anywhere = pl.BlockSpec(memory_space=pl.ANY)
    return pl.pallas_call(
        finish_kernel,
        in_specs=[pl.BlockSpec(memory_space=pltpu.SMEM), anywhere, anywhere],
        out_specs=anywhere,
        out_shape=jax.ShapeDtypeStruct(own.shape, jnp.float32),
        scratch_shapes=[pltpu.VMEM(own.shape, jnp.float32), pltpu.SemaphoreType.DMA((2,))],
        compiler_params=pltpu.CompilerParams(vmem_limit_bytes=VMEM_LIMIT // 6),
        cost_estimate=pl.CostEstimate(
            flops=6_000_000_000, bytes_accessed=8 * own.size, transcendentals=0
        ),
        name="finished",
    )(core, own, other)


def core_kernel(counts, snaps, me_ref, own_ref, other_ref, *refs):
    halves, (mode_ref, *outs), basis = refs[: 2 * len(counts)], refs[2 * len(counts) : -1], refs[-1]
    me, part = me_ref[0], own_ref.shape[0] // NB
    basis[...] = jnp.where(me_ref[1] == 0, own_ref[...], other_ref[...])
    mode_ref[...] = basis[...].T
    turned = [basis[pl.ds(pl.multiple_of((me ^ b) * part, part), part), :] for b in range(NB)]
    high, low = split(jnp.concatenate(turned, axis=0).T)
    weights = jnp.concatenate([high, low], axis=1)
    cell = 0
    for c, count in enumerate(counts):
        high_ref, low_ref = halves[2 * c : 2 * c + 2]
        for i in range(count):
            rows = slice(snaps * i, snaps * i + snaps)
            both = contract(high_ref[rows, :], weights, ((1,), (0,)))
            more = contract(low_ref[rows, :], high, ((1,), (0,)))
            core = (both[:, :W] + (both[:, W:] + more)).T
            for b in range(NB):
                outs[b][cell] = core[part * b : part * b + part, :]
            cell += 1


def core_parts(place, own_basis, other_basis, halves, counts, snaps):
    rank, size = own_basis.shape
    cells = sum(counts)
    operands = [half for pair in halves for half in pair]
    vmem = pl.BlockSpec(memory_space=pltpu.VMEM)
    return pl.pallas_call(
        lambda *refs: core_kernel(counts, snaps, *refs),
        in_specs=[pl.BlockSpec(memory_space=pltpu.SMEM)] + [vmem] * (2 + len(operands)),
        out_specs=[vmem] * (1 + NB),
        out_shape=[jax.ShapeDtypeStruct((size, rank), jnp.float32)]
        + [jax.ShapeDtypeStruct((cells, rank // NB, snaps), jnp.float32)] * NB,
        scratch_shapes=[pltpu.VMEM((rank, size), jnp.float32)],
        compiler_params=pltpu.CompilerParams(vmem_limit_bytes=SMALL),
        cost_estimate=pl.CostEstimate(
            flops=6 * cells * snaps * size * rank,
            bytes_accessed=5 * cells * snaps * size,
            transcendentals=0,
        ),
        name="core_parts",
    )(place, own_basis, other_basis, *operands)


def placed_kernel(me_ref, *refs):
    parts, (out_ref, held, sems) = refs[:NB], refs[NB:]
    arrivals = [
        pltpu.make_async_copy(part, held.at[b], sems.at[b]) for b, part in enumerate(parts)
    ]
    leaving = [
        pltpu.make_async_copy(held.at[b], out_ref.at[me_ref[0] ^ b], sems.at[NB + b])
        for b in range(NB)
    ]
    for copy in arrivals:
        copy.start()
    for arrival, copy in zip(arrivals, leaving):
        arrival.wait()
        copy.start()
    for copy in leaving:
        copy.wait()


def placed(me, parts):
    anywhere = pl.BlockSpec(memory_space=pl.ANY)
    return pl.pallas_call(
        placed_kernel,
        in_specs=[pl.BlockSpec(memory_space=pltpu.SMEM)] + [anywhere] * NB,
        out_specs=anywhere,
        out_shape=jax.ShapeDtypeStruct((NB, *parts[0].shape), jnp.float32),
        scratch_shapes=[
            pltpu.VMEM((NB, *parts[0].shape), jnp.float32),
            pltpu.SemaphoreType.DMA((2 * NB,)),
        ],
        compiler_params=pltpu.CompilerParams(vmem_limit_bytes=VMEM_LIMIT // 6),
        name="placed",
    )(me, *parts)


def exchanged(block, axis, bits):
    count = lax.axis_size(axis)
    return lax.ppermute(block, axis, [(i, i ^ bits) for i in range(count)])


def summed_over_devices(part):
    half = part.shape[0] // 2
    core = lax.axis_index("core")
    keep = lax.dynamic_slice_in_dim(part, core * half, half, 0)
    send = lax.dynamic_slice_in_dim(part, (1 - core) * half, half, 0)
    own = keep + exchanged(send, "core", 1)
    shares = lax.all_to_all(
        own.reshape(NB, half // NB, W), "x", split_axis=0, concat_axis=0, tiled=True
    )
    own = (shares[0] + shares[1]) + (shares[2] + shares[3])
    two, one, three = (exchanged(own, "y", bits) for bits in (2, 1, 3))
    own = (own + one) + (two + three)
    own = own + exchanged(own, "z", 1)
    four, two, six = (exchanged(own, "z", bits) for bits in (4, 2, 6))
    own = (own + two) + (four + six)
    copies = jnp.broadcast_to(own[None], (NB, *own.shape))
    whole = lax.all_to_all(copies, "x", split_axis=0, concat_axis=0, tiled=True)
    whole = whole.reshape(half, W)
    return lax.all_gather(whole, "core", axis=0, tiled=True)


def local(soil_heat_field, seed_subspace):
    cells, snaps, width = soil_heat_field.shape
    devices = lax.axis_size(("x", "y", "z", "core"))
    me, core = lax.axis_index("x"), lax.axis_index("core")
    place = jnp.stack([me, core]).astype(jnp.int32)
    field = soil_heat_field.reshape(NB, cells // NB, snaps, width)
    scale = 1.0 / (cells // NB * snaps * devices)
    counts = COUNTS

    arrived, start, later = [], 0, field
    for count in counts:
        got = {}
        for bits in (2, 1, 3):
            send = lax.dynamic_slice(later, (me ^ bits, start, 0, 0), (1, count, snaps, width))[0]
            got[bits] = exchanged(send, "x", bits)
            later, _ = lax.optimization_barrier((later, send))
        arrived.append([got[bits] for bits in (1, 2, 3)])
        start += count
    gram, high, low = gram_blocks(place, field, counts, arrived, scale)

    gram = summed_over_devices(gram.reshape(-1, W)).reshape(gram.shape)
    basis, triangle = basis_or_triangle(place[1:], gram, seed_subspace.T)
    other_basis = exchanged(basis, "core", 1)
    triangle, other_basis = lax.optimization_barrier((triangle, other_basis))
    other_triangle = exchanged(triangle, "core", 1)
    mode_factor, *parts = core_parts(
        place, basis, other_basis, [(high, low)], [cells // NB], snaps
    )
    sent = {bits: exchanged(parts[bits], "x", bits) for bits in (2, 1, 3)}
    triangle = finished(place[1:], triangle, other_triangle)
    own_part, triangle = lax.optimization_barrier((parts[0], triangle))
    core_tensor = placed(place, [own_part] + [sent[bits] for bits in (1, 2, 3)])
    core_tensor = core_tensor.reshape(cells, -1, snaps).transpose(0, 2, 1)
    return (core_tensor, mode_factor, triangle)


def solution(mesh):
    fine = Mesh(mesh.devices.reshape(4, -1, 8, 2), ("x", "y", "z", "core"))
    cell = ("y", "z", "core")
    return jax.shard_map(
        local,
        mesh=fine,
        in_specs=(P(cell, None, "x"), P()),
        out_specs=(P(cell, None, "x"), P(), P()),
        check_vma=False,
    )
```
